512 devices in a mesh: ctx: 32 (over z_lo, y), grp: 16 (over x, z_hi, core).
Axes of the slice: x: 4, y: 4, z: 16 (z_hi: 2, z_lo: 8; z = z_hi * 8 + z_lo), core: 2. Of those that a mesh axis runs over, the one named last changes fastest.
Arguments:
- q_nope: bfloat16 [256, 128, 128], P(None, 'ctx'), may hold values from -6 to 6
- q_rope: bfloat16 [256, 128, 64], P(None, 'ctx'), may hold values from -720 to 720
- w_uk: bfloat16 [128, 128, 512], P('ctx'), may hold values from -0.5 to 0.5
- w_uv: bfloat16 [128, 512, 128], P('ctx'), may hold values from -0.375 to 0.375
- prompt: bfloat16 [6144, 576], P('grp'), may hold values from -12 to 12
- w_out: bfloat16 [16384, 7168], P('ctx', 'grp'), may hold values from -0.0625 to 0.0625
- residual: bfloat16 [256, 7168], P('ctx', 'grp'), may hold values from -3 to 3
- routes: int32 [256, 8], P('ctx'), may hold values from 0 to 31, all different within a row; in each aligned block of 8 rows (0 to 7, 8 to 15, ...) at most 4 rows name the same one
- route_scores: float32 [256, 8], P('ctx'), may hold values from 0.05 to 1
- expert_gate: bfloat16 [32, 7168, 1024], P('ctx', 'grp'), may hold values from -0.0625 to 0.0625
- expert_up: bfloat16 [32, 7168, 1024], P('ctx', 'grp'), may hold values from -0.0625 to 0.0625
- expert_down: bfloat16 [32, 1024, 7168], P('ctx', None, 'grp'), may hold values from -0.1875 to 0.1875
Outputs:
- layer_out: bfloat16 [256, 7168], P('ctx', 'grp')
The draws below stay inside these ranges and needn't reach their ends.
Inputs may be any that keep to these rules, and one draw needn't show every extreme that they name: `routes`: in each aligned block of 8 rows no expert is named by more than 4 rows, a bound that some block reaches; the 8 experts of a row differ.
All inputs are finite; a program needn't handle non-finite values.
Results may differ from the reference program's by a relative error of at most 0.0163.
Values may be sent and summed in bfloat16 or wider, within the bound.
A program may use at most 64 MiB of HBM per device.

```python
import math
import jax
import jax.numpy as jnp
import numpy as np
from jax import lax

D = 7168
H = 128
NOPE = 128
ROPE = 64
LAT = 512
VDIM = 128
TOPK = 8
FF = 1024
ROW_DEV = 8
EXPERTS = 32
CAP = 4
ROWS = 256
PROMPT = 6144


def prompt_table(key):
    base_key = jax.random.fold_in(key, 11)
    first_key = jax.random.fold_in(base_key, 0)
    table = jnp.clip(jax.random.normal(first_key, (PROMPT, LAT + ROPE), jnp.float32), -6.0, 6.0)
    return table


def draw_prompt(key, part):
    return prompt_table(key).astype(jnp.bfloat16)


def draw_q_rope(key, part):
    first_key = jax.random.fold_in(jax.random.fold_in(key, 23), 0)
    noise = jnp.clip(jax.random.normal(first_key, (ROWS, H, ROPE), jnp.float32), -6.0, 6.0)
    return noise.astype(jnp.bfloat16)


def block_levels(stream_key, shape, pieces, least, largest):
    def one(position, parts):
        draws = jax.random.uniform(jax.random.fold_in(jax.random.fold_in(stream_key, 6), position), (parts,), jnp.float32, least / len(pieces), largest / len(pieces))
        return jnp.repeat(jnp.exp(draws), shape[position] // parts).reshape((-1,) + (1,) * (len(shape) - position - 1))

    factor_of = one(*pieces[0])
    for cut in pieces[1:]:
        factor_of = factor_of * one(*cut)
    return factor_of


def assign_block(stream_key, own, number, rows, number_of, top, most, lean):
    sequence = jax.random.permutation(stream_key, number_of)
    heavy_load, common = portions_of(number_of, rows * top, most, lean, True), portions_of(number_of, rows * top, most, lean, False)
    places = jnp.arange(number_of)

    def named(sizes, turn):
        used = int((sizes > 0).sum())
        fixed = max(1, used // 4)
        moved = fixed + (places - fixed + turn * (used - fixed)) % max(1, number_of - fixed)
        return jnp.zeros((number_of,), jnp.int32).at[sequence[jnp.where(places < fixed, places, moved)]].set(jnp.asarray(sizes, jnp.int32))

    sizes = jnp.where(number % 4 == 0, named(heavy_load, number // 4), named(common, number - number // 4 - 1))
    mixed = jax.random.permutation(jax.random.fold_in(own, 3), number_of)
    donor, receiver = mixed[0:number_of // 2 * 2:2], mixed[1:number_of // 2 * 2:2]
    room = jnp.minimum(sizes[donor] - 1, most - sizes[receiver]) // 2
    room = jnp.where((donor == sequence[0]) | (receiver == sequence[0]) | (sizes[receiver] == 0), 0, jnp.maximum(room, 0))
    moved = jax.random.randint(jax.random.fold_in(own, 4), (number_of // 2,), 0, 1 << 20) % (room + 1)
    sizes = sizes.at[donor].add(-moved).at[receiver].add(moved)
    items = jnp.searchsorted(jnp.cumsum(sizes), jnp.arange(rows * top), side="right").astype(jnp.int32)
    grid = items.reshape(top, rows).T
    grid = grid[jax.random.permutation(jax.random.fold_in(own, 1), rows)]
    turn = jax.random.randint(jax.random.fold_in(own, 2), (rows, 1), 0, top)
    return jnp.take_along_axis(grid, (jnp.arange(top)[None, :] + turn) % top, axis=1)


def portions_of(number_of, total, limit, skew, full):
    weights = [(1 << 20) // math.isqrt(standing ** skew) + 1 for standing in range(1, number_of + 1)]
    largest = limit if full else min(limit, max(-(-total // number_of), total * weights[0] // sum(weights)))
    least = 1 if total - largest >= number_of - 1 else 0
    counts, surplus = [largest] + [least] * (number_of - 1), total - largest - least * (number_of - 1)
    while surplus > 0:
        movable = [i for i in range(1, number_of) if counts[i] < largest] or [i for i in range(1, number_of) if counts[i] < limit]
        pool, remaining = sum([weights[i] for i in movable]), surplus
        for i in movable:
            more = min(limit - counts[i], max(1, remaining * weights[i] // pool), surplus)
            counts[i] = counts[i] + more
            surplus = surplus - more
    return np.array(counts)


def bell_draw(stream_key, extent, spread, reach, pieces=(), held_as=jnp.bfloat16):
    values = jax.random.normal(stream_key, extent, jnp.float32) * spread
    if len(pieces) > 0:
        values = block_levels(stream_key, extent, pieces, -0.22, 0.18) * values
    return jnp.clip(values, min=-reach, max=reach).astype(held_as)


def setup_inputs(seed: int = 0) -> dict:
    streams_of = jax.random.split(jax.random.key(seed), 13)
    q_nope = bell_draw(streams_of[0], (ROWS, H, NOPE), 1.0, 6.0, ((1, 32),))
    q_rope = draw_q_rope(jax.random.fold_in(streams_of[12], 71), 0)
    w_uk = bell_draw(streams_of[2], (H, NOPE, LAT), NOPE ** -0.5, 0.5, ((0, 32),))
    w_uv = bell_draw(streams_of[3], (H, LAT, VDIM), (LAT // 2) ** -0.5, 0.375, ((0, 32),))
    prompt = draw_prompt(jax.random.fold_in(streams_of[12], 71), 0)
    w_out = bell_draw(streams_of[5], (H * VDIM, D), (H * VDIM // 2) ** -0.5, 0.0625, ((0, 32), (1, 16)))
    residual = bell_draw(streams_of[6], (ROWS, D), 0.5, 3.0, ((0, 32), (1, 16)))
    routes_keys = jax.random.split(jax.random.fold_in(streams_of[7], 1), ROWS // ROW_DEV)
    routes_turns = jax.random.permutation(jax.random.fold_in(streams_of[7], 3), ROWS // ROW_DEV)
    routes = jax.vmap(lambda own, number: assign_block(jax.random.fold_in(streams_of[7], 2), own, number, ROW_DEV, EXPERTS, TOPK, CAP, 2))(routes_keys, routes_turns).reshape((ROWS, TOPK))
    route_scores = jnp.clip(0.05 + 0.95 * jax.random.uniform(streams_of[8], (ROWS, TOPK), jnp.float32) ** block_levels(streams_of[8], (ROWS, TOPK), ((0, 32),), -0.2, 0.2), 0.05, 1.0)
    expert_gate = bell_draw(streams_of[9], (EXPERTS, D, FF), D ** -0.5, 0.0625, ((0, 32), (1, 16)))
    expert_up = bell_draw(streams_of[10], (EXPERTS, D, FF), D ** -0.5, 0.0625, ((0, 32), (1, 16)))
    expert_down = bell_draw(streams_of[11], (EXPERTS, FF, D), FF ** -0.5, 0.1875, ((0, 32), (2, 16)))
    return {"q_nope": q_nope, "q_rope": q_rope, "w_uk": w_uk, "w_uv": w_uv, "prompt": prompt, "w_out": w_out, "residual": residual, "routes": routes, "route_scores": route_scores, "expert_gate": expert_gate, "expert_up": expert_up, "expert_down": expert_down}


route_factor = 2.5


def reference(q_nope, q_rope, w_uk, w_uv, prompt, w_out, residual, routes, route_scores, expert_gate, expert_up, expert_down):
    score_scale = (NOPE + ROPE) ** -0.5
    q_latent = jnp.einsum("rhn,hnl->rhl", q_nope.astype(jnp.float32), w_uk.astype(jnp.float32)).astype(jnp.bfloat16)
    queries = jnp.concatenate([q_latent, q_rope], axis=-1)
    latents = prompt[:, :LAT]

    def one_head(packed):
        head_query, head_uv = packed
        scores = jnp.dot(head_query, prompt.T, preferred_element_type=jnp.float32) * score_scale
        top_score = jnp.max(scores, axis=-1, keepdims=True)
        raised = jnp.exp(scores - top_score)
        denominator = jnp.sum(raised, axis=-1, keepdims=True)
        weighted = jnp.dot(raised.astype(jnp.bfloat16), latents, preferred_element_type=jnp.float32)
        values = jnp.dot(weighted, head_uv.astype(jnp.float32), precision=lax.Precision.HIGHEST)
        return (values / denominator).astype(jnp.bfloat16)

    heads_out = lax.map(one_head, (jnp.transpose(queries, (1, 0, 2)), w_uv))
    attended = jnp.transpose(heads_out, (1, 0, 2)).reshape(ROWS, H * VDIM)
    hidden = residual.astype(jnp.float32) + jnp.dot(attended, w_out, preferred_element_type=jnp.float32)
    moe_input = hidden.astype(jnp.bfloat16)
    gate_weights = route_factor * route_scores / jnp.sum(route_scores, axis=-1, keepdims=True)

    def one_expert(running, packed):
        expert_index, w_gate, w_up, w_down = packed
        row_weight = jnp.sum(jnp.where(routes == expert_index, gate_weights, 0.0), axis=-1)
        gate_sum = jnp.dot(moe_input, w_gate, preferred_element_type=jnp.float32)
        up_sum = jnp.dot(moe_input, w_up, preferred_element_type=jnp.float32)
        activated = (jax.nn.silu(gate_sum) * up_sum).astype(jnp.bfloat16)
        result = jnp.dot(activated, w_down, preferred_element_type=jnp.float32).astype(jnp.bfloat16)
        return running + row_weight[:, None] * result.astype(jnp.float32), None

    expert_ids = jnp.arange(EXPERTS, dtype=jnp.int32)
    combined = lax.scan(one_expert, jnp.zeros((ROWS, D), jnp.float32), (expert_ids, expert_gate, expert_up, expert_down))[0]
    return (hidden + combined).astype(jnp.bfloat16)
```

```python
import jax
import jax.numpy as jnp
from jax import lax
from jax.experimental import pallas as pl
from jax.experimental.pallas import tpu as pltpu
from jax.sharding import PartitionSpec as P

NOPE = 128
ROPE = 64
LAT = 512
VDIM = 128
CAP = 4
TOPK = 8
FF = 1024
ROWS = 256
HEADS = 4
KEYS = 384
COLS = 448
LANES = 128
PAD = 512
QS = PAD // LANES
ROW_DEV = 8
NZ, NY, NX = 8, 4, 4
NCTX = NZ * NY
SLOTS = NCTX * CAP
ROUTE_FACTOR = 2.5
FAR_FIRST = (2, 1, 3, 0)
F32 = jnp.float32
BF16 = jnp.bfloat16
MESH = pl.DeviceIdType.MESH


def dot(a, b, ca, cb):
    return lax.dot_general(a, b, (((ca,), (cb,)), ((), ())), preferred_element_type=F32)


def split(a):
    high = a.astype(BF16)
    return high, (a - high.astype(F32)).astype(BF16)


def kernel(
    qn, qr, w_uk, w_uv, prompt, residual, routes, scores, w_out_hbm, wg_hbm, wu_hbm, wd_hbm,
    out,
    w_out, wgu, wd, perm, perm_t,
    obuf, lse, o_recv, l_recv, zh_send, zh_recv, zl_send, zl_recv, att,
    proj, pbuf, p_recv, zbuf, z_recv, res_pad, disp, arrived,
    gu, gu_recv, gz_send, gz_recv, act, down, ret, ret_recv,
    load_sem, o_sem, l_sem, zh_sem, ag_sem, y_sem, z_sem, d_sem, g_sem, gz_sem, act_sem, r_sem,
):
    me_c = lax.axis_index("ctx")
    me_g = lax.axis_index("grp")
    z, y = me_c // NY, me_c % NY
    x, zh, core = me_g // 4, (me_g // 2) % 2, me_g % 2
    me_q = x * 2 + core
    partner = {"grp": x * 4 + (1 - zh) * 2 + core}

    def near(d, c):
        return {"grp": ((x + d) % NX) * 4 + zh * 2 + c}

    barrier = pltpu.get_barrier_semaphore()
    for d in range(NX):
        if d:
            for c in range(2):
                pl.semaphore_signal(barrier, inc=1, device_id=near(d, c), device_id_type=MESH)
    pl.semaphore_signal(barrier, inc=1, device_id=near(0, 1 - core), device_id_type=MESH)
    pl.semaphore_signal(barrier, inc=1, device_id=partner, device_id_type=MESH)

    def greet(d, carry):
        pl.semaphore_signal(
            barrier, inc=1, device_id={"ctx": (me_c + d) % NCTX}, device_id_type=MESH
        )
        return carry

    lax.fori_loop(1, NCTX, greet, 0)

    loads = [
        pltpu.make_async_copy(w_out_hbm, w_out, load_sem.at[0]),
        pltpu.make_async_copy(wg_hbm, wgu.at[pl.ds(0, COLS), pl.ds(0, FF)], load_sem.at[1]),
        pltpu.make_async_copy(wu_hbm, wgu.at[pl.ds(0, COLS), pl.ds(FF, FF)], load_sem.at[2]),
        pltpu.make_async_copy(wd_hbm, wd, load_sem.at[3]),
    ]
    for load in loads:
        load.start()
    sent = []

    def send(src, dst, sems, n, at, device):
        copy = pltpu.make_async_remote_copy(
            src_ref=src, dst_ref=dst, send_sem=sems.at[0, n], recv_sem=sems.at[1, at],
            device_id=device, device_id_type=MESH,
        )
        copy.start()
        sent.append((src, sems, n))

    def arrive(dst, sems, at):
        pltpu.make_async_remote_copy(
            src_ref=dst, dst_ref=dst, send_sem=sems.at[0, at], recv_sem=sems.at[1, at],
            device_id=partner, device_id_type=MESH,
        ).wait_recv()

    scale = (NOPE + ROPE) ** -0.5
    latents = prompt[:, 0:LAT]
    rotated = prompt[:, LAT : LAT + ROPE]
    for step, d in enumerate(FAR_FIRST):
        h = (x + d) % NX
        q_latent = dot(qn[h], w_uk[h], 1, 0).astype(BF16)
        s = (dot(latents, q_latent, 1, 1) + dot(rotated, qr[h], 1, 1)) * scale
        top = jnp.max(s, axis=0, keepdims=True)
        raised = jnp.exp(s - top)
        total = jnp.sum(raised, axis=0, keepdims=True)
        weighted = dot(latents, raised.astype(BF16), 0, 0)
        high, low = split(weighted)
        values = dot(w_uv[h], high, 0, 0) + dot(w_uv[h], low, 0, 0)
        o = (values / total).astype(BF16)
        obuf[h] = o.reshape(2, VDIM // 2, ROWS)
        lse[h] = jnp.broadcast_to(top + jnp.log(total), (8, ROWS))
        if step == 0:
            pl.semaphore_wait(barrier, 2 * NX - 1 + 1 + NCTX - 1)
        for c in range(2) if d else (1 - core,):
            send(obuf.at[h, c], o_recv.at[d * 2 + core], o_sem, d * 2 + c, d * 2 + core, near(d, c))
            send(lse.at[h], l_recv.at[d * 2 + core], l_sem, d * 2 + c, d * 2 + core, near(d, c))
        if d == 0:
            o_recv[core] = obuf[h, core]
            l_recv[core] = lse[h]

    wgu[COLS:PAD, :] = jnp.zeros((PAD - COLS, 2 * FF), BF16)
    slot = lax.broadcasted_iota(jnp.int32, (PAD, PAD), 0)
    place = lax.broadcasted_iota(jnp.int32, (PAD, PAD), 1)

    def place_of(k):
        k2 = k % SLOTS
        return (k2 // CAP) * (QS * CAP) + (k // SLOTS) * CAP + k2 % CAP

    perm[...] = jnp.where(place_of(slot) == place, 1.0, 0.0).astype(BF16)
    perm_t[...] = jnp.where(place_of(place) == slot, 1.0, 0.0).astype(BF16)
    res_pad[...] = jnp.zeros((ROW_DEV, PAD), F32)
    res_pad[:, 0:COLS] = residual[...].astype(F32)
    proj[:, PAD - LANES : PAD] = jnp.zeros((ROWS, LANES), F32)
    down[:, PAD - LANES : PAD] = jnp.zeros((SLOTS, LANES), F32)

    lane = lax.broadcasted_iota(jnp.int32, (ROW_DEV, PAD), 1)
    expert_of = lane // (QS * CAP)
    scored = scores[...]
    gate_weights = ROUTE_FACTOR * scored / jnp.sum(scored, axis=1, keepdims=True)
    chosen = jnp.zeros((ROW_DEV, PAD), F32)
    weight = jnp.zeros((ROW_DEV, PAD), F32)
    for k in range(TOPK):
        hit = routes[:, k : k + 1] == expert_of
        chosen = chosen + jnp.where(hit, 1.0, 0.0)
        weight = weight + jnp.where(hit, gate_weights[:, k : k + 1], 0.0)
    row = lax.broadcasted_iota(jnp.int32, (ROW_DEV, PAD), 0)
    before = jnp.zeros((ROW_DEV, PAD), F32)
    for r in range(ROW_DEV - 1):
        before = before + jnp.where(row > r, chosen[r : r + 1, :], 0.0)
    picked = jnp.where(before == (lane % CAP).astype(F32), chosen, 0.0)
    block_of = (lane // CAP) % QS
    pick = jnp.concatenate([jnp.where(block_of == q, picked, 0.0) for q in range(QS)], axis=0)
    pick_weight = jnp.concatenate(
        [jnp.where(block_of == q, picked * weight, 0.0) for q in range(QS)], axis=0
    )

    for d in FAR_FIRST:
        for c in range(2) if d else (1 - core,):
            arrive(o_recv.at[d * 2 + c], o_sem, d * 2 + c)
            arrive(l_recv.at[d * 2 + c], l_sem, d * 2 + c)

    def merge(outs, sums):
        top = sums[0]
        for v in sums[1:]:
            top = jnp.maximum(top, v)
        scaled = [jnp.exp(v - top) for v in sums]
        total = scaled[0]
        for v in scaled[1:]:
            total = total + v
        o = jnp.zeros(outs[0].shape, F32)
        for v, s in zip(outs, scaled):
            o = o + v.astype(F32) * s
        return o / total, top + jnp.log(total)

    o, l = merge([o_recv[i] for i in range(2 * NX)], [l_recv[i, 0:1, :] for i in range(2 * NX)])
    zh_send[...] = o.astype(BF16)
    zl_send[...] = jnp.broadcast_to(l, (8, ROWS))
    send(zh_send, zh_recv, zh_sem, 0, 0, partner)
    send(zl_send, zl_recv, zh_sem, 1, 1, partner)
    arrive(zh_recv, zh_sem, 0)
    arrive(zl_recv, zh_sem, 1)
    o, _ = merge([zh_send[...], zh_recv[...]], [l, zl_recv[0:1, :]])
    att[me_q] = o.astype(BF16)
    for d in FAR_FIRST:
        for c in range(2) if d else (1 - core,):
            send(att.at[me_q], att.at[me_q], ag_sem, d * 2 + c, d * 2 + core, near(d, c))
    for d in FAR_FIRST:
        for c in range(2) if d else (1 - core,):
            arrive(att.at[((x + NX - d) % NX) * 2 + c], ag_sem, d * 2 + c)

    loads[0].wait()
    proj[:, 0:COLS] = dot(att[...].reshape(HEADS * VDIM, ROWS), w_out[...], 0, 0)
    for to in range(NY):
        parts = []
        for q in range(QS):
            part = proj[:, q * LANES : (q + 1) * LANES].reshape(NZ, NY, ROW_DEV, LANES)
            parts.append(part[:, to])
        pbuf[to] = jnp.stack(parts, axis=1).reshape(NZ * QS * ROW_DEV, LANES).astype(BF16)
    for d in (2, 1, 3):
        to = (y + d) % NY
        send(pbuf.at[to], p_recv.at[d], y_sem, d, d, {"ctx": z * NY + to})
    total = pbuf[y].astype(F32)
    for d in (1, 3, 2):
        arrive(p_recv.at[d], y_sem, d)
        total = total + p_recv[d].astype(F32)
    zbuf[...] = total.reshape(NZ, QS * ROW_DEV, LANES).astype(BF16)
    for d in (4, 3, 5, 2, 6, 1, 7):
        to = (z + d) % NZ
        send(zbuf.at[to], z_recv.at[d], z_sem, d, d, {"ctx": to * NY + y})
    hidden = jnp.concatenate([res_pad[:, q * LANES : (q + 1) * LANES] for q in range(QS)], axis=0)
    hidden = hidden + zbuf[z].astype(F32)
    for d in (1, 7, 2, 6, 3, 5, 4):
        arrive(z_recv.at[d], z_sem, d)
        hidden = hidden + z_recv[d].astype(F32)

    outgoing = dot(pick.astype(BF16), hidden.astype(BF16), 0, 0).astype(BF16)
    disp[...] = outgoing.reshape(NCTX, QS * CAP, LANES)
    arrived[me_c] = disp[me_c]

    def to_all(src, dst, sems):
        def copy(d):
            to = (me_c + d) % NCTX
            return pltpu.make_async_remote_copy(
                src_ref=src.at[to], dst_ref=dst.at[me_c], send_sem=sems.at[0, d],
                recv_sem=sems.at[1, d], device_id={"ctx": to}, device_id_type=MESH,
            )

        def start(d, carry):
            copy(d).start()
            return carry

        def finish(d, carry):
            arrive(dst.at[(me_c + NCTX - d) % NCTX], sems, d)
            return carry

        def leave(d, carry):
            copy(d).wait_send()
            return carry

        return [lambda f=f: lax.fori_loop(1, NCTX, f, 0) for f in (start, finish, leave)]

    start, finish, leave_disp = to_all(disp, arrived, d_sem)
    start()
    loads[1].wait()
    loads[2].wait()
    finish()
    rows = dot(perm[...], arrived[...].reshape(PAD, LANES), 1, 0).astype(BF16)
    rows = jnp.concatenate([rows[q * SLOTS : (q + 1) * SLOTS] for q in range(QS)], axis=1)

    wide = 2 * LANES
    for d in FAR_FIRST:
        first = pl.multiple_of(((x + d) % NX) * wide, wide)
        gate = dot(rows, wgu[:, pl.ds(first, wide)], 1, 0).astype(BF16)
        up = dot(rows, wgu[:, pl.ds(FF + first, wide)], 1, 0).astype(BF16)
        for c in range(2):
            gu[d, c, 0:SLOTS, :] = gate[:, c * LANES : (c + 1) * LANES]
            gu[d, c, SLOTS : 2 * SLOTS, :] = up[:, c * LANES : (c + 1) * LANES]
        for c in range(2) if d else (1 - core,):
            send(gu.at[d, c], gu_recv.at[d * 2 + core], g_sem, d * 2 + c, d * 2 + core, near(d, c))
    sums = gu[0, core].astype(F32)
    for d in (0, 1, 3, 2):
        for c in range(2) if d else (1 - core,):
            arrive(gu_recv.at[d * 2 + c], g_sem, d * 2 + c)
            sums = sums + gu_recv[d * 2 + c].astype(F32)
    gz_send[...] = sums.astype(BF16)
    send(gz_send, gz_recv, gz_sem, 0, 0, partner)
    arrive(gz_recv, gz_sem, 0)
    sums = sums + gz_recv[...].astype(F32)
    gate, up = sums[0:SLOTS], sums[SLOTS : 2 * SLOTS]
    act[me_q] = (gate / (1.0 + jnp.exp(-gate)) * up).astype(BF16)
    for d in FAR_FIRST:
        for c in range(2) if d else (1 - core,):
            send(act.at[me_q], act.at[me_q], act_sem, d * 2 + c, d * 2 + core, near(d, c))
    loads[3].wait()
    for d in (0, 1, 3, 2):
        for c in range(2) if d else (1 - core,):
            arrive(act.at[((x + NX - d) % NX) * 2 + c], act_sem, d * 2 + c)
    hidden_units = jnp.concatenate([act[q] for q in range(2 * NX)], axis=1)
    down[:, 0:COLS] = dot(hidden_units, wd[...], 1, 0)

    result = jnp.concatenate([down[:, q * LANES : (q + 1) * LANES] for q in range(QS)], axis=0)
    packed = dot(perm_t[...], result.astype(BF16), 1, 0).astype(BF16)
    ret[...] = packed.reshape(NCTX, QS * CAP, LANES)
    ret_recv[me_c] = ret[me_c]
    start, finish, leave_ret = to_all(ret, ret_recv, r_sem)
    start()
    finish()
    returned = ret_recv[...].reshape(PAD, LANES)
    high, low = split(pick_weight)
    final = (hidden + dot(high, returned, 1, 0) + dot(low, returned, 1, 0)).astype(BF16)
    for q in range(QS):
        width = min(LANES, COLS - q * LANES)
        out[:, q * LANES : q * LANES + width] = final[q * ROW_DEV : (q + 1) * ROW_DEV, 0:width]

    for src, sems, n in sent:
        pltpu.make_async_remote_copy(
            src_ref=src, dst_ref=src, send_sem=sems.at[0, n], recv_sem=sems.at[1, n],
            device_id=partner, device_id_type=MESH,
        ).wait_send()
    leave_disp()
    leave_ret()


def per_device(
    q_nope, q_rope, w_uk, w_uv, prompt, w_out, residual, routes, route_scores,
    expert_gate, expert_up, expert_down,
):
    vmem, hbm = pl.BlockSpec(memory_space=pltpu.VMEM), pl.BlockSpec(memory_space=pl.ANY)
    dma = pltpu.SemaphoreType.DMA
    near = 2 * NX
    half = VDIM // 2
    scratch = [
        ((HEADS * VDIM, COLS), BF16),
        ((PAD, 2 * FF), BF16),
        ((FF, COLS), BF16),
        ((PAD, PAD), BF16),
        ((PAD, PAD), BF16),
        ((HEADS, 2, half, ROWS), BF16),
        ((HEADS, 8, ROWS), F32),
        ((near, half, ROWS), BF16),
        ((near, 8, ROWS), F32),
        ((half, ROWS), BF16),
        ((half, ROWS), BF16),
        ((8, ROWS), F32),
        ((8, ROWS), F32),
        ((near, half, ROWS), BF16),
        ((ROWS, PAD), F32),
        ((NY, ROWS, LANES), BF16),
        ((NY, ROWS, LANES), BF16),
        ((NZ, QS * ROW_DEV, LANES), BF16),
        ((NZ, QS * ROW_DEV, LANES), BF16),
        ((ROW_DEV, PAD), F32),
        ((NCTX, QS * CAP, LANES), BF16),
        ((NCTX, QS * CAP, LANES), BF16),
        ((NX, 2, 2 * SLOTS, LANES), BF16),
        ((near, 2 * SLOTS, LANES), BF16),
        ((2 * SLOTS, LANES), BF16),
        ((2 * SLOTS, LANES), BF16),
        ((near, SLOTS, LANES), BF16),
        ((SLOTS, PAD), F32),
        ((NCTX, QS * CAP, LANES), BF16),
        ((NCTX, QS * CAP, LANES), BF16),
    ]
    sems = [(4,)] + [(2, n) for n in (near, near, 2, near, NY, NZ, NCTX, near, 1, near, NCTX)]
    return pl.pallas_call(
        kernel,
        out_shape=jax.ShapeDtypeStruct((ROW_DEV, COLS), BF16),
        in_specs=[vmem] * 8 + [hbm] * 4,
        out_specs=vmem,
        scratch_shapes=[pltpu.VMEM(*s) for s in scratch] + [dma(s) for s in sems],
        compiler_params=pltpu.CompilerParams(
            collective_id=0, has_side_effects=True, vmem_limit_bytes=48 * 2**20
        ),
        name="layer",
    )(
        jnp.transpose(q_nope, (1, 0, 2)),
        jnp.transpose(q_rope, (1, 0, 2)),
        w_uk, w_uv, prompt, residual, routes, route_scores, w_out,
        expert_gate[0], expert_up[0], expert_down[0],
    )


def solution(mesh):
    in_specs = (
        P(None, "ctx", None),
        P(None, "ctx", None),
        P("ctx", None, None),
        P("ctx", None, None),
        P("grp", None),
        P("ctx", "grp"),
        P("ctx", "grp"),
        P("ctx", None),
        P("ctx", None),
        P("ctx", "grp", None),
        P("ctx", "grp", None),
        P("ctx", None, "grp"),
    )
    return jax.shard_map(
        per_device, mesh=mesh, in_specs=in_specs, out_specs=P("ctx", "grp"), check_vma=False
    )
```

```python
import jax
import jax.numpy as jnp
from jax import lax
from jax.experimental import pallas as pl
from jax.experimental.pallas import tpu as pltpu
from jax.sharding import PartitionSpec as P

NOPE = 128
ROPE = 64
LAT = 512
VDIM = 128
CAP = 4
TOPK = 8
FF = 1024
ROWS = 256
HEADS = 4
KEYS = 384
COLS = 448
LANES = 128
PAD = 512
QS = PAD // LANES
ROW_DEV = 8
NZ, NY, NX = 8, 4, 4
NCTX = NZ * NY
SLOTS = NCTX * CAP
ROUTE_FACTOR = 2.5
FAR_FIRST = (2, 1, 3, 0)
F32 = jnp.float32
BF16 = jnp.bfloat16
MESH = pl.DeviceIdType.MESH


def dot(a, b, ca, cb):
    return lax.dot_general(a, b, (((ca,), (cb,)), ((), ())), preferred_element_type=F32)


def split(a):
    high = a.astype(BF16)
    return high, (a - high.astype(F32)).astype(BF16)


def kernel(
    residual, routes, scores,
    qn_hbm, qr_hbm, w_uk_hbm, w_uv_hbm, prompt_hbm, w_out_hbm, wg_hbm, wu_hbm, wd_hbm,
    out,
    qn, q_wide, qr, w_uk, w_uv, prompt, keys,
    w_out, wgu, wd, perm, perm_t,
    obuf, lse, o_recv, l_recv, zh_send, zh_recv, zl_send, zl_recv, att,
    proj, pbuf, p_recv, zbuf, z_recv, res_pad, disp, arrived,
    gu, gu_recv, gz_send, gz_recv, act, down, ret, ret_recv,
    load_sem, o_sem, l_sem, zh_sem, ag_sem, y_sem, z_sem, d_sem, g_sem, gz_sem, act_sem, r_sem,
):
    me_c = lax.axis_index("ctx")
    me_g = lax.axis_index("grp")
    z, y = me_c // NY, me_c % NY
    x, zh, core = me_g // 4, (me_g // 2) % 2, me_g % 2
    me_q = x * 2 + core
    partner = {"grp": x * 4 + (1 - zh) * 2 + core}

    def near(d, c):
        return {"grp": ((x + d) % NX) * 4 + zh * 2 + c}

    pairs = (
        (prompt_hbm, prompt),
        (qn_hbm, qn),
        (w_uk_hbm, w_uk),
        (qr_hbm, qr),
        (w_uv_hbm, w_uv),
        (w_out_hbm, w_out),
        (wg_hbm, wgu.at[pl.ds(0, COLS), pl.ds(0, FF)]),
        (wu_hbm, wgu.at[pl.ds(0, COLS), pl.ds(FF, FF)]),
        (wd_hbm, wd),
    )
    loads = [pltpu.make_async_copy(a, b, load_sem.at[i]) for i, (a, b) in enumerate(pairs)]
    for load in loads:
        load.start()
    barrier = pltpu.get_barrier_semaphore()
    for d in range(NX):
        if d:
            for c in range(2):
                pl.semaphore_signal(barrier, inc=1, device_id=near(d, c), device_id_type=MESH)
    pl.semaphore_signal(barrier, inc=1, device_id=near(0, 1 - core), device_id_type=MESH)
    pl.semaphore_signal(barrier, inc=1, device_id=partner, device_id_type=MESH)

    def greet(d, carry):
        pl.semaphore_signal(
            barrier, inc=1, device_id={"ctx": (me_c + d) % NCTX}, device_id_type=MESH
        )
        return carry

    lax.fori_loop(1, NCTX, greet, 0)

    sent = []

    def send(src, dst, sems, n, at, device):
        copy = pltpu.make_async_remote_copy(
            src_ref=src, dst_ref=dst, send_sem=sems.at[0, n], recv_sem=sems.at[1, at],
            device_id=device, device_id_type=MESH,
        )
        copy.start()
        sent.append((src, sems, n))

    def arrive(dst, sems, at):
        pltpu.make_async_remote_copy(
            src_ref=dst, dst_ref=dst, send_sem=sems.at[0, at], recv_sem=sems.at[1, at],
            device_id=partner, device_id_type=MESH,
        ).wait_recv()

    scale = (NOPE + ROPE) ** -0.5
    for load in loads[0:5]:
        load.wait()
    keys[...] = prompt[...].T
    q_wide[...] = qn[...].astype(F32)
    for step, d in enumerate(FAR_FIRST):
        h = (x + d) % NX
        q = q_wide[pl.ds(h, ROWS, stride=HEADS), :].astype(BF16)
        queries = jnp.concatenate([dot(w_uk[h], q, 0, 1).astype(BF16), qr[h]], axis=0)
        s = dot(keys[...], queries, 1, 0) * scale
        top = jnp.max(s, axis=0, keepdims=True)
        raised = jnp.exp(s - top)
        total = jnp.sum(raised, axis=0, keepdims=True)
        weighted = dot(prompt[0:LAT, :], raised.astype(BF16), 1, 0)
        high, low = split(weighted)
        values = dot(w_uv[h], high, 0, 0) + dot(w_uv[h], low, 0, 0)
        o = (values / total).astype(BF16)
        obuf[h] = o.reshape(2, VDIM // 2, ROWS)
        lse[h] = jnp.broadcast_to(top + jnp.log(total), (8, ROWS))
        if step == 0:
            pl.semaphore_wait(barrier, 2 * NX - 1 + 1 + NCTX - 1)
        for c in range(2) if d else (1 - core,):
            send(obuf.at[h, c], o_recv.at[d * 2 + core], o_sem, d * 2 + c, d * 2 + core, near(d, c))
            send(lse.at[h], l_recv.at[d * 2 + core], l_sem, d * 2 + c, d * 2 + core, near(d, c))
        if d == 0:
            o_recv[core] = obuf[h, core]
            l_recv[core] = lse[h]

    wgu[COLS:PAD, :] = jnp.zeros((PAD - COLS, 2 * FF), BF16)
    slot = lax.broadcasted_iota(jnp.int32, (PAD, PAD), 0)
    place = lax.broadcasted_iota(jnp.int32, (PAD, PAD), 1)

    def place_of(k):
        k2 = k % SLOTS
        return (k2 // CAP) * (QS * CAP) + (k // SLOTS) * CAP + k2 % CAP

    perm[...] = jnp.where(place_of(slot) == place, 1.0, 0.0).astype(BF16)
    perm_t[...] = jnp.where(place_of(place) == slot, 1.0, 0.0).astype(BF16)
    res_pad[...] = jnp.zeros((ROW_DEV, PAD), F32)
    res_pad[:, 0:COLS] = residual[...].astype(F32)
    proj[:, PAD - LANES : PAD] = jnp.zeros((ROWS, LANES), F32)
    down[:, PAD - LANES : PAD] = jnp.zeros((SLOTS, LANES), F32)

    lane = lax.broadcasted_iota(jnp.int32, (ROW_DEV, PAD), 1)
    expert_of = lane // (QS * CAP)
    scored = scores[...]
    gate_weights = ROUTE_FACTOR * scored / jnp.sum(scored, axis=1, keepdims=True)
    chosen = jnp.zeros((ROW_DEV, PAD), F32)
    weight = jnp.zeros((ROW_DEV, PAD), F32)
    for k in range(TOPK):
        hit = routes[:, k : k + 1] == expert_of
        chosen = chosen + jnp.where(hit, 1.0, 0.0)
        weight = weight + jnp.where(hit, gate_weights[:, k : k + 1], 0.0)
    row = lax.broadcasted_iota(jnp.int32, (ROW_DEV, PAD), 0)
    before = jnp.zeros((ROW_DEV, PAD), F32)
    for r in range(ROW_DEV - 1):
        before = before + jnp.where(row > r, chosen[r : r + 1, :], 0.0)
    picked = jnp.where(before == (lane % CAP).astype(F32), chosen, 0.0)
    block_of = (lane // CAP) % QS
    pick = jnp.concatenate([jnp.where(block_of == q, picked, 0.0) for q in range(QS)], axis=0)
    pick_weight = jnp.concatenate(
        [jnp.where(block_of == q, picked * weight, 0.0) for q in range(QS)], axis=0
    )

    for d in FAR_FIRST:
        for c in range(2) if d else (1 - core,):
            arrive(o_recv.at[d * 2 + c], o_sem, d * 2 + c)
            arrive(l_recv.at[d * 2 + c], l_sem, d * 2 + c)

    def merge(outs, sums):
        top = sums[0]
        for v in sums[1:]:
            top = jnp.maximum(top, v)
        scaled = [jnp.exp(v - top) for v in sums]
        total = scaled[0]
        for v in scaled[1:]:
            total = total + v
        o = jnp.zeros(outs[0].shape, F32)
        for v, s in zip(outs, scaled):
            o = o + v.astype(F32) * s
        return o / total, top + jnp.log(total)

    o, l = merge([o_recv[i] for i in range(2 * NX)], [l_recv[i, 0:1, :] for i in range(2 * NX)])
    zh_send[...] = o.astype(BF16)
    zl_send[...] = jnp.broadcast_to(l, (8, ROWS))
    send(zh_send, zh_recv, zh_sem, 0, 0, partner)
    send(zl_send, zl_recv, zh_sem, 1, 1, partner)
    arrive(zh_recv, zh_sem, 0)
    arrive(zl_recv, zh_sem, 1)
    o, _ = merge([zh_send[...], zh_recv[...]], [l, zl_recv[0:1, :]])
    att[me_q] = o.astype(BF16)
    for d in FAR_FIRST:
        for c in range(2) if d else (1 - core,):
            send(att.at[me_q], att.at[me_q], ag_sem, d * 2 + c, d * 2 + core, near(d, c))
    for d in FAR_FIRST:
        for c in range(2) if d else (1 - core,):
            arrive(att.at[((x + NX - d) % NX) * 2 + c], ag_sem, d * 2 + c)

    loads[5].wait()
    proj[:, 0:COLS] = dot(att[...].reshape(HEADS * VDIM, ROWS), w_out[...], 0, 1)
    for to in range(NY):
        parts = []
        for q in range(QS):
            part = proj[:, q * LANES : (q + 1) * LANES].reshape(NZ, NY, ROW_DEV, LANES)
            parts.append(part[:, to])
        pbuf[to] = jnp.stack(parts, axis=1).reshape(NZ * QS * ROW_DEV, LANES).astype(BF16)
    for d in (2, 1, 3):
        to = (y + d) % NY
        send(pbuf.at[to], p_recv.at[d], y_sem, d, d, {"ctx": z * NY + to})
    total = pbuf[y].astype(F32)
    for d in (1, 3, 2):
        arrive(p_recv.at[d], y_sem, d)
        total = total + p_recv[d].astype(F32)
    zbuf[...] = total.reshape(NZ, QS * ROW_DEV, LANES).astype(BF16)
    for d in (4, 3, 5, 2, 6, 1, 7):
        to = (z + d) % NZ
        send(zbuf.at[to], z_recv.at[d], z_sem, d, d, {"ctx": to * NY + y})
    hidden = jnp.concatenate([res_pad[:, q * LANES : (q + 1) * LANES] for q in range(QS)], axis=0)
    hidden = hidden + zbuf[z].astype(F32)
    for d in (1, 7, 2, 6, 3, 5, 4):
        arrive(z_recv.at[d], z_sem, d)
        hidden = hidden + z_recv[d].astype(F32)

    outgoing = dot(pick.astype(BF16), hidden.astype(BF16), 0, 0).astype(BF16)
    disp[...] = outgoing.reshape(NCTX, QS * CAP, LANES)
    arrived[me_c] = disp[me_c]

    def to_all(src, dst, sems):
        def copy(d):
            to = (me_c + d) % NCTX
            return pltpu.make_async_remote_copy(
                src_ref=src.at[to], dst_ref=dst.at[me_c], send_sem=sems.at[0, d],
                recv_sem=sems.at[1, d], device_id={"ctx": to}, device_id_type=MESH,
            )

        def start(d, carry):
            copy(d).start()
            return carry

        def finish(d, carry):
            arrive(dst.at[(me_c + NCTX - d) % NCTX], sems, d)
            return carry

        def leave(d, carry):
            copy(d).wait_send()
            return carry

        return [lambda f=f: lax.fori_loop(1, NCTX, f, 0) for f in (start, finish, leave)]

    start, finish, leave_disp = to_all(disp, arrived, d_sem)
    start()
    loads[6].wait()
    loads[7].wait()
    finish()
    rows = dot(perm[...], arrived[...].reshape(PAD, LANES), 1, 0).astype(BF16)
    rows = jnp.concatenate([rows[q * SLOTS : (q + 1) * SLOTS] for q in range(QS)], axis=1)

    wide = 2 * LANES
    for d in FAR_FIRST:
        first = pl.multiple_of(((x + d) % NX) * wide, wide)
        gate = dot(rows, wgu[:, pl.ds(first, wide)], 1, 0).astype(BF16)
        up = dot(rows, wgu[:, pl.ds(FF + first, wide)], 1, 0).astype(BF16)
        for c in range(2):
            gu[d, c, 0:SLOTS, :] = gate[:, c * LANES : (c + 1) * LANES]
            gu[d, c, SLOTS : 2 * SLOTS, :] = up[:, c * LANES : (c + 1) * LANES]
        for c in range(2) if d else (1 - core,):
            send(gu.at[d, c], gu_recv.at[d * 2 + core], g_sem, d * 2 + c, d * 2 + core, near(d, c))
    sums = gu[0, core].astype(F32)
    for d in (0, 1, 3, 2):
        for c in range(2) if d else (1 - core,):
            arrive(gu_recv.at[d * 2 + c], g_sem, d * 2 + c)
            sums = sums + gu_recv[d * 2 + c].astype(F32)
    gz_send[...] = sums.astype(BF16)
    send(gz_send, gz_recv, gz_sem, 0, 0, partner)
    arrive(gz_recv, gz_sem, 0)
    sums = sums + gz_recv[...].astype(F32)
    gate, up = sums[0:SLOTS], sums[SLOTS : 2 * SLOTS]
    act[me_q] = (gate / (1.0 + jnp.exp(-gate)) * up).astype(BF16)
    for d in FAR_FIRST:
        for c in range(2) if d else (1 - core,):
            send(act.at[me_q], act.at[me_q], act_sem, d * 2 + c, d * 2 + core, near(d, c))
    loads[8].wait()
    for d in (0, 1, 3, 2):
        for c in range(2) if d else (1 - core,):
            arrive(act.at[((x + NX - d) % NX) * 2 + c], act_sem, d * 2 + c)
    hidden_units = jnp.concatenate([act[q] for q in range(2 * NX)], axis=1)
    down[:, 0:COLS] = dot(hidden_units, wd[...], 1, 1)

    result = jnp.concatenate([down[:, q * LANES : (q + 1) * LANES] for q in range(QS)], axis=0)
    packed = dot(perm_t[...], result.astype(BF16), 1, 0).astype(BF16)
    ret[...] = packed.reshape(NCTX, QS * CAP, LANES)
    ret_recv[me_c] = ret[me_c]
    start, finish, leave_ret = to_all(ret, ret_recv, r_sem)
    start()
    finish()
    returned = ret_recv[...].reshape(PAD, LANES)
    high, low = split(pick_weight)
    final = (hidden + dot(high, returned, 1, 0) + dot(low, returned, 1, 0)).astype(BF16)
    for q in range(QS):
        width = min(LANES, COLS - q * LANES)
        out[:, q * LANES : q * LANES + width] = final[q * ROW_DEV : (q + 1) * ROW_DEV, 0:width]

    for src, sems, n in sent:
        pltpu.make_async_remote_copy(
            src_ref=src, dst_ref=src, send_sem=sems.at[0, n], recv_sem=sems.at[1, n],
            device_id=partner, device_id_type=MESH,
        ).wait_send()
    leave_disp()
    leave_ret()


def per_device(
    q_nope, q_rope, w_uk, w_uv, prompt, w_out, residual, routes, route_scores,
    expert_gate, expert_up, expert_down,
):
    vmem, hbm = pl.BlockSpec(memory_space=pltpu.VMEM), pl.BlockSpec(memory_space=pl.ANY)
    dma = pltpu.SemaphoreType.DMA
    near = 2 * NX
    half = VDIM // 2
    scratch = [
        ((ROWS * HEADS, NOPE), BF16),
        ((ROWS * HEADS, NOPE), F32),
        ((HEADS, ROPE, ROWS), BF16),
        ((HEADS, NOPE, LAT), BF16),
        ((HEADS, LAT, VDIM), BF16),
        ((LAT + ROPE, KEYS), BF16),
        ((KEYS, LAT + ROPE), BF16),
        ((COLS, HEADS * VDIM), BF16),
        ((PAD, 2 * FF), BF16),
        ((COLS, FF), BF16),
        ((PAD, PAD), BF16),
        ((PAD, PAD), BF16),
        ((HEADS, 2, half, ROWS), BF16),
        ((HEADS, 8, ROWS), F32),
        ((near, half, ROWS), BF16),
        ((near, 8, ROWS), F32),
        ((half, ROWS), BF16),
        ((half, ROWS), BF16),
        ((8, ROWS), F32),
        ((8, ROWS), F32),
        ((near, half, ROWS), BF16),
        ((ROWS, PAD), F32),
        ((NY, ROWS, LANES), BF16),
        ((NY, ROWS, LANES), BF16),
        ((NZ, QS * ROW_DEV, LANES), BF16),
        ((NZ, QS * ROW_DEV, LANES), BF16),
        ((ROW_DEV, PAD), F32),
        ((NCTX, QS * CAP, LANES), BF16),
        ((NCTX, QS * CAP, LANES), BF16),
        ((NX, 2, 2 * SLOTS, LANES), BF16),
        ((near, 2 * SLOTS, LANES), BF16),
        ((2 * SLOTS, LANES), BF16),
        ((2 * SLOTS, LANES), BF16),
        ((near, SLOTS, LANES), BF16),
        ((SLOTS, PAD), F32),
        ((NCTX, QS * CAP, LANES), BF16),
        ((NCTX, QS * CAP, LANES), BF16),
    ]
    sems = [(9,)] + [(2, n) for n in (near, near, 2, near, NY, NZ, NCTX, near, 1, near, NCTX)]
    return pl.pallas_call(
        kernel,
        out_shape=jax.ShapeDtypeStruct((ROW_DEV, COLS), BF16),
        in_specs=[vmem] * 3 + [hbm] * 9,
        out_specs=vmem,
        scratch_shapes=[pltpu.VMEM(*s) for s in scratch] + [dma(s) for s in sems],
        compiler_params=pltpu.CompilerParams(
            collective_id=0, has_side_effects=True, vmem_limit_bytes=60 * 2**20
        ),
        name="layer",
    )(
        residual, routes, route_scores,
        q_nope.reshape(ROWS * HEADS, NOPE), jnp.transpose(q_rope, (1, 2, 0)), w_uk, w_uv, prompt.T,
        w_out.T, expert_gate[0], expert_up[0], expert_down[0].T,
    )


def solution(mesh):
    in_specs = (
        P(None, "ctx", None),
        P(None, "ctx", None),
        P("ctx", None, None),
        P("ctx", None, None),
        P("grp", None),
        P("ctx", "grp"),
        P("ctx", "grp"),
        P("ctx", None),
        P("ctx", None),
        P("ctx", "grp", None),
        P("ctx", "grp", None),
        P("ctx", None, "grp"),
    )
    return jax.shard_map(
        per_device, mesh=mesh, in_specs=in_specs, out_specs=P("ctx", "grp"), check_vma=False
    )
```

```python
import jax
import jax.numpy as jnp
from jax import lax
from jax.experimental import pallas as pl
from jax.experimental.pallas import tpu as pltpu
from jax.sharding import PartitionSpec as P

NOPE = 128
ROPE = 64
LAT = 512
VDIM = 128
CAP = 4
TOPK = 8
FF = 1024
ROWS = 256
HEADS = 4
KEYS = 384
COLS = 448
LANES = 128
PAD = 512
QS = PAD // LANES
ROW_DEV = 8
NZ, NY, NX = 8, 4, 4
NCTX = NZ * NY
SLOTS = NCTX * CAP
ROUTE_FACTOR = 2.5
FAR_FIRST = (2, 1, 3, 0)
OFFSETS = [(dz, dy) for dz in (4, 3, 5, 2, 6, 1, 7, 0) for dy in FAR_FIRST][:-1]
F32 = jnp.float32
BF16 = jnp.bfloat16
MESH = pl.DeviceIdType.MESH


def dot(a, b, ca, cb):
    return lax.dot_general(a, b, (((ca,), (cb,)), ((), ())), preferred_element_type=F32)


def split(a):
    high = a.astype(BF16)
    return high, (a - high.astype(F32)).astype(BF16)


def kernel(
    residual, routes, scores,
    qn_hbm, qr_hbm, w_uk_hbm, w_uv_hbm, prompt_hbm, w_out_hbm, wg_hbm, wu_hbm, wd_hbm,
    out,
    qn, q_wide, qr, w_uk, w_uv, prompt, keys,
    w_out, wgu, wd, perm, perm_t,
    obuf, lse, o_recv, l_recv, zh_send, zh_recv, zl_send, zl_recv, att,
    proj, pbuf, p_recv, zbuf, z_recv, res_pad, disp, arrived,
    gu_own, gu_send, gu_recv, gx_send, gx_recv, gz_send, gz_recv, act, down, ret, ret_recv,
    load_sem, o_sem, l_sem, zh_sem, ag_sem, y_sem, z_sem, d_sem, gs_sem, g_sem, gz_sem, act_sem, r_sem,
):
    me_c = lax.axis_index("ctx")
    me_g = lax.axis_index("grp")
    z, y = me_c // NY, me_c % NY
    x, zh, core = me_g // 4, (me_g // 2) % 2, me_g % 2
    me_q = x * 2 + core
    partner = {"grp": x * 4 + (1 - zh) * 2 + core}

    def near(d, c):
        return {"grp": ((x + d) % NX) * 4 + zh * 2 + c}

    pairs = (
        (prompt_hbm, prompt),
        (qn_hbm, qn),
        (w_uk_hbm, w_uk),
        (qr_hbm, qr),
        (w_uv_hbm, w_uv),
        (w_out_hbm, w_out),
        (wg_hbm, wgu.at[pl.ds(0, COLS), pl.ds(0, FF)]),
        (wu_hbm, wgu.at[pl.ds(0, COLS), pl.ds(FF, FF)]),
        (wd_hbm, wd),
    )
    loads = [pltpu.make_async_copy(a, b, load_sem.at[i]) for i, (a, b) in enumerate(pairs)]
    for load in loads:
        load.start()
    barrier = pltpu.get_barrier_semaphore()
    sibling = near(0, 1 - core)
    others = [((z + dz) % NZ) * NY + (y + dy) % NY for dz, dy in OFFSETS]
    sources = [((z + NZ - dz) % NZ) * NY + (y + NY - dy) % NY for dz, dy in OFFSETS]
    greeted = [partner] + [{"ctx": c} for c in others]
    greeted += [near(d, c) for d in FAR_FIRST[:3] for c in range(2)] + [sibling]
    for device in greeted:
        pl.semaphore_signal(barrier, inc=1, device_id=device, device_id_type=MESH)
    sent = []

    def send(src, dst, sems, n, at, device):
        copy = pltpu.make_async_remote_copy(
            src_ref=src, dst_ref=dst, send_sem=sems.at[0, n], recv_sem=sems.at[1, at],
            device_id=device, device_id_type=MESH,
        )
        copy.start()
        sent.append((src, sems, n))

    def arrive(dst, sems, at):
        pltpu.make_async_remote_copy(
            src_ref=dst, dst_ref=dst, send_sem=sems.at[0, at], recv_sem=sems.at[1, at],
            device_id=partner, device_id_type=MESH,
        ).wait_recv()

    def spread(buf, sems):
        for d in (2, 1, 3):
            send(buf.at[me_q], buf.at[me_q], sems, d, d, near(d, core))
        send(buf.at[me_q], buf.at[me_q], sems, NX, NX, sibling)
        for d in (1, 3, 2):
            got = ((x + NX - d) % NX) * 2 + core
            arrive(buf.at[got], sems, d)
            send(buf.at[got], buf.at[got], sems, NX + d, NX + d, sibling)
        for d in (0, 1, 3, 2):
            arrive(buf.at[((x + NX - d) % NX) * 2 + 1 - core], sems, NX + d)

    scale = (NOPE + ROPE) ** -0.5
    for load in loads[0:5]:
        load.wait()
    keys[...] = prompt[...].T
    q_wide[...] = qn[...].astype(F32)
    for h in range(HEADS):
        q = q_wide[pl.ds(h, ROWS, stride=HEADS), :].astype(BF16)
        queries = jnp.concatenate([dot(w_uk[h], q, 0, 1).astype(BF16), qr[h]], axis=0)
        s = dot(keys[...], queries, 1, 0) * scale
        top = jnp.max(s, axis=0, keepdims=True)
        raised = jnp.exp(s - top)
        total = jnp.sum(raised, axis=0, keepdims=True)
        weighted = dot(prompt[0:LAT, :], raised.astype(BF16), 1, 0)
        high, low = split(weighted)
        values = dot(w_uv[h], high, 0, 0) + dot(w_uv[h], low, 0, 0)
        o = (values / total).astype(BF16)
        obuf[h] = o.reshape(2, VDIM // 2, ROWS)
        lse[h] = jnp.broadcast_to(top + jnp.log(total), (8, ROWS))
    pl.semaphore_wait(barrier, len(greeted))
    for d in FAR_FIRST:
        h = (x + d) % NX
        for c in range(2) if d else (1 - core,):
            send(obuf.at[h, c], o_recv.at[d * 2 + core], o_sem, d * 2 + c, d * 2 + core, near(d, c))
            send(lse.at[h], l_recv.at[d * 2 + core], l_sem, d * 2 + c, d * 2 + core, near(d, c))
    o_recv[core] = obuf[x, core]
    l_recv[core] = lse[x]

    wgu[COLS:PAD, :] = jnp.zeros((PAD - COLS, 2 * FF), BF16)
    slot = lax.broadcasted_iota(jnp.int32, (PAD, PAD), 0)
    place = lax.broadcasted_iota(jnp.int32, (PAD, PAD), 1)

    def place_of(k):
        k2 = k % SLOTS
        return (k2 // CAP) * (QS * CAP) + (k // SLOTS) * CAP + k2 % CAP

    perm[...] = jnp.where(place_of(slot) == place, 1.0, 0.0).astype(BF16)
    perm_t[...] = jnp.where(place_of(place) == slot, 1.0, 0.0).astype(BF16)
    res_pad[...] = jnp.zeros((ROW_DEV, PAD), F32)
    res_pad[:, 0:COLS] = residual[...].astype(F32)
    proj[:, PAD - LANES : PAD] = jnp.zeros((ROWS, LANES), F32)
    down[:, PAD - LANES : PAD] = jnp.zeros((SLOTS, LANES), F32)

    lane = lax.broadcasted_iota(jnp.int32, (ROW_DEV, PAD), 1)
    expert_of = lane // (QS * CAP)
    scored = scores[...]
    gate_weights = ROUTE_FACTOR * scored / jnp.sum(scored, axis=1, keepdims=True)
    chosen = jnp.zeros((ROW_DEV, PAD), F32)
    weight = jnp.zeros((ROW_DEV, PAD), F32)
    for k in range(TOPK):
        hit = routes[:, k : k + 1] == expert_of
        chosen = chosen + jnp.where(hit, 1.0, 0.0)
        weight = weight + jnp.where(hit, gate_weights[:, k : k + 1], 0.0)
    row = lax.broadcasted_iota(jnp.int32, (ROW_DEV, PAD), 0)
    before = jnp.zeros((ROW_DEV, PAD), F32)
    for r in range(ROW_DEV - 1):
        before = before + jnp.where(row > r, chosen[r : r + 1, :], 0.0)
    picked = jnp.where(before == (lane % CAP).astype(F32), chosen, 0.0)
    block_of = (lane // CAP) % QS
    pick = jnp.concatenate([jnp.where(block_of == q, picked, 0.0) for q in range(QS)], axis=0)
    pick_weight = jnp.concatenate(
        [jnp.where(block_of == q, picked * weight, 0.0) for q in range(QS)], axis=0
    )

    for d in FAR_FIRST:
        for c in range(2) if d else (1 - core,):
            arrive(o_recv.at[d * 2 + c], o_sem, d * 2 + c)
            arrive(l_recv.at[d * 2 + c], l_sem, d * 2 + c)

    def merge(outs, sums):
        top = sums[0]
        for v in sums[1:]:
            top = jnp.maximum(top, v)
        scaled = [jnp.exp(v - top) for v in sums]
        total = scaled[0]
        for v in scaled[1:]:
            total = total + v
        o = jnp.zeros(outs[0].shape, F32)
        for v, s in zip(outs, scaled):
            o = o + v.astype(F32) * s
        return o / total, top + jnp.log(total)

    o, l = merge([o_recv[i] for i in range(2 * NX)], [l_recv[i, 0:1, :] for i in range(2 * NX)])
    zh_send[...] = o.astype(BF16)
    zl_send[...] = jnp.broadcast_to(l, (8, ROWS))
    send(zh_send, zh_recv, zh_sem, 0, 0, partner)
    send(zl_send, zl_recv, zh_sem, 1, 1, partner)
    arrive(zh_recv, zh_sem, 0)
    arrive(zl_recv, zh_sem, 1)
    o, _ = merge([zh_send[...], zh_recv[...]], [l, zl_recv[0:1, :]])
    att[me_q] = o.astype(BF16)
    spread(att, ag_sem)

    loads[5].wait()
    proj[:, 0:COLS] = dot(att[...].reshape(HEADS * VDIM, ROWS), w_out[...], 0, 1)
    for to in range(NY):
        parts = []
        for q in range(QS):
            part = proj[:, q * LANES : (q + 1) * LANES].reshape(NZ, NY, ROW_DEV, LANES)
            parts.append(part[:, to])
        pbuf[to] = jnp.stack(parts, axis=1).reshape(NZ * QS * ROW_DEV, LANES).astype(BF16)
    for d in (2, 1, 3):
        to = (y + d) % NY
        send(pbuf.at[to], p_recv.at[d], y_sem, d, d, {"ctx": z * NY + to})
    total = pbuf[y].astype(F32)
    for d in (1, 3, 2):
        arrive(p_recv.at[d], y_sem, d)
        total = total + p_recv[d].astype(F32)
    zbuf[...] = total.reshape(NZ, QS * ROW_DEV, LANES).astype(BF16)
    for d in (4, 3, 5, 2, 6, 1, 7):
        to = (z + d) % NZ
        send(zbuf.at[to], z_recv.at[d], z_sem, d, d, {"ctx": to * NY + y})
    hidden = jnp.concatenate([res_pad[:, q * LANES : (q + 1) * LANES] for q in range(QS)], axis=0)
    hidden = hidden + zbuf[z].astype(F32)
    for d in (1, 7, 2, 6, 3, 5, 4):
        arrive(z_recv.at[d], z_sem, d)
        hidden = hidden + z_recv[d].astype(F32)

    outgoing = dot(pick.astype(BF16), hidden.astype(BF16), 0, 0).astype(BF16)
    disp[...] = outgoing.reshape(NCTX, QS * CAP, LANES)
    def to_all(src, dst, sems):
        dst[me_c] = src[me_c]
        for n, to in enumerate(others):
            send(src.at[to], dst.at[me_c], sems, n, n, {"ctx": to})

    def from_all(dst, sems):
        for n, source in enumerate(sources):
            arrive(dst.at[source], sems, n)

    to_all(disp, arrived, d_sem)
    loads[6].wait()
    loads[7].wait()
    from_all(arrived, d_sem)
    rows = dot(perm[...], arrived[...].reshape(PAD, LANES), 1, 0).astype(BF16)
    rows = jnp.concatenate([rows[q * SLOTS : (q + 1) * SLOTS] for q in range(QS)], axis=1)

    wide = 2 * LANES
    for d in FAR_FIRST:
        first = pl.multiple_of(((x + d) % NX) * wide, wide)
        gate = dot(rows, wgu[:, pl.ds(first, wide)], 1, 0)
        up = dot(rows, wgu[:, pl.ds(FF + first, wide)], 1, 0)
        even = jnp.concatenate([gate[:, 0:LANES], up[:, 0:LANES]], axis=0)
        odd = jnp.concatenate([gate[:, LANES:wide], up[:, LANES:wide]], axis=0)
        gu_own[d] = jnp.where(core == 0, even, odd)
        gu_send[d] = jnp.where(core == 0, odd, even).astype(BF16)
        send(gu_send.at[d], gu_recv.at[d], gs_sem, d, d, sibling)
    for d in (2, 1, 3):
        arrive(gu_recv.at[d], gs_sem, d)
        gx_send[d] = (gu_own[d] + gu_recv[d].astype(F32)).astype(BF16)
        send(gx_send.at[d], gx_recv.at[d], g_sem, d, d, near(d, core))
    arrive(gu_recv.at[0], gs_sem, 0)
    sums = gu_own[0] + gu_recv[0].astype(F32)
    for d in (1, 3, 2):
        arrive(gx_recv.at[d], g_sem, d)
        sums = sums + gx_recv[d].astype(F32)
    gz_send[...] = sums.astype(BF16)
    send(gz_send, gz_recv, gz_sem, 0, 0, partner)
    arrive(gz_recv, gz_sem, 0)
    sums = sums + gz_recv[...].astype(F32)
    gate, up = sums[0:SLOTS], sums[SLOTS : 2 * SLOTS]
    act[me_q] = (gate / (1.0 + jnp.exp(-gate)) * up).astype(BF16)
    loads[8].wait()
    spread(act, act_sem)
    hidden_units = jnp.concatenate([act[q] for q in range(2 * NX)], axis=1)
    down[:, 0:COLS] = dot(hidden_units, wd[...], 1, 1)

    result = jnp.concatenate([down[:, q * LANES : (q + 1) * LANES] for q in range(QS)], axis=0)
    packed = dot(perm_t[...], result.astype(BF16), 1, 0).astype(BF16)
    ret[...] = packed.reshape(NCTX, QS * CAP, LANES)
    to_all(ret, ret_recv, r_sem)
    from_all(ret_recv, r_sem)
    returned = ret_recv[...].reshape(PAD, LANES)
    high, low = split(pick_weight)
    final = (hidden + dot(high, returned, 1, 0) + dot(low, returned, 1, 0)).astype(BF16)
    for q in range(QS):
        width = min(LANES, COLS - q * LANES)
        out[:, q * LANES : q * LANES + width] = final[q * ROW_DEV : (q + 1) * ROW_DEV, 0:width]

    for src, sems, n in sent:
        pltpu.make_async_remote_copy(
            src_ref=src, dst_ref=src, send_sem=sems.at[0, n], recv_sem=sems.at[1, n],
            device_id=partner, device_id_type=MESH,
        ).wait_send()


def per_device(
    q_nope, q_rope, w_uk, w_uv, prompt, w_out, residual, routes, route_scores,
    expert_gate, expert_up, expert_down,
):
    vmem, hbm = pl.BlockSpec(memory_space=pltpu.VMEM), pl.BlockSpec(memory_space=pl.ANY)
    dma = pltpu.SemaphoreType.DMA
    near = 2 * NX
    half = VDIM // 2
    scratch = [
        ((ROWS * HEADS, NOPE), BF16),
        ((ROWS * HEADS, NOPE), F32),
        ((HEADS, ROPE, ROWS), BF16),
        ((HEADS, NOPE, LAT), BF16),
        ((HEADS, LAT, VDIM), BF16),
        ((LAT + ROPE, KEYS), BF16),
        ((KEYS, LAT + ROPE), BF16),
        ((COLS, HEADS * VDIM), BF16),
        ((PAD, 2 * FF), BF16),
        ((COLS, FF), BF16),
        ((PAD, PAD), BF16),
        ((PAD, PAD), BF16),
        ((HEADS, 2, half, ROWS), BF16),
        ((HEADS, 8, ROWS), F32),
        ((near, half, ROWS), BF16),
        ((near, 8, ROWS), F32),
        ((half, ROWS), BF16),
        ((half, ROWS), BF16),
        ((8, ROWS), F32),
        ((8, ROWS), F32),
        ((near, half, ROWS), BF16),
        ((ROWS, PAD), F32),
        ((NY, ROWS, LANES), BF16),
        ((NY, ROWS, LANES), BF16),
        ((NZ, QS * ROW_DEV, LANES), BF16),
        ((NZ, QS * ROW_DEV, LANES), BF16),
        ((ROW_DEV, PAD), F32),
        ((NCTX, QS * CAP, LANES), BF16),
        ((NCTX, QS * CAP, LANES), BF16),
        ((NX, 2 * SLOTS, LANES), F32),
        ((NX, 2 * SLOTS, LANES), BF16),
        ((NX, 2 * SLOTS, LANES), BF16),
        ((NX, 2 * SLOTS, LANES), BF16),
        ((NX, 2 * SLOTS, LANES), BF16),
        ((2 * SLOTS, LANES), BF16),
        ((2 * SLOTS, LANES), BF16),
        ((near, SLOTS, LANES), BF16),
        ((SLOTS, PAD), F32),
        ((NCTX, QS * CAP, LANES), BF16),
        ((NCTX, QS * CAP, LANES), BF16),
    ]
    sems = [(9,)] + [(2, n) for n in (near, near, 2, near, NY, NZ, NCTX, NX, NX, 1, near, NCTX)]
    return pl.pallas_call(
        kernel,
        out_shape=pltpu.VMEM((ROW_DEV, COLS), BF16),
        in_specs=[vmem] * 3 + [hbm] * 9,
        out_specs=vmem,
        scratch_shapes=[pltpu.VMEM(*s) for s in scratch] + [dma(s) for s in sems],
        compiler_params=pltpu.CompilerParams(
            collective_id=0, has_side_effects=True, vmem_limit_bytes=60 * 2**20
        ),
        name="layer",
    )(
        residual, routes, route_scores,
        q_nope.reshape(ROWS * HEADS, NOPE), jnp.transpose(q_rope, (1, 2, 0)), w_uk, w_uv, prompt.T,
        w_out.T, expert_gate[0], expert_up[0], expert_down[0].T,
    )


def solution(mesh):
    in_specs = (
        P(None, "ctx", None),
        P(None, "ctx", None),
        P("ctx", None, None),
        P("ctx", None, None),
        P("grp", None),
        P("ctx", "grp"),
        P("ctx", "grp"),
        P("ctx", None),
        P("ctx", None),
        P("ctx", "grp", None),
        P("ctx", "grp", None),
        P("ctx", None, "grp"),
    )
    return jax.shard_map(
        per_device, mesh=mesh, in_specs=in_specs, out_specs=P("ctx", "grp"), check_vma=False
    )
```

```python
import jax
import jax.numpy as jnp
from jax import lax
from jax.experimental import pallas as pl
from jax.experimental.pallas import tpu as pltpu
from jax.sharding import PartitionSpec as P

NOPE = 128
ROPE = 64
LAT = 512
VDIM = 128
CAP = 4
TOPK = 8
FF = 1024
ROWS = 256
HEADS = 4
KEYS = 384
COLS = 448
LANES = 128
PAD = 512
QS = PAD // LANES
ROW_DEV = 8
NZ, NY, NX = 8, 4, 4
NCTX = NZ * NY
SLOTS = NCTX * CAP
ROUTE_FACTOR = 2.5
FAR_FIRST = (2, 1, 3, 0)
OFFSETS = [(dz, dy) for dz in (4, 3, 5, 2, 6, 1, 7, 0) for dy in FAR_FIRST][:-1]
F32 = jnp.float32
BF16 = jnp.bfloat16
MESH = pl.DeviceIdType.MESH


def dot(a, b, ca, cb):
    return lax.dot_general(a, b, (((ca,), (cb,)), ((), ())), preferred_element_type=F32)


def split(a):
    high = a.astype(BF16)
    return high, (a - high.astype(F32)).astype(BF16)


def kernel(
    residual, routes, scores,
    qn_hbm, qr_hbm, w_uk_hbm, w_uv_hbm, prompt_hbm, w_out_hbm, wg_hbm, wu_hbm, wd_hbm,
    out,
    qn, q_wide, qr, w_uk, w_uv, prompt, keys,
    w_out, w_out_t, wgu, wd, wd_t, perm, perm_t,
    obuf, lse, o_recv, l_recv, zh_send, zh_recv, zl_send, zl_recv, att,
    proj, pbuf, p_recv, zbuf, z_recv, res_pad, disp, arrived,
    gu_own, gu_send, gu_recv, gx_send, gx_recv, gz_send, gz_recv, act, down, ret, ret_recv,
    load_sem, o_sem, l_sem, zh_sem, ag_sem, y_sem, z_sem, d_sem, gs_sem, g_sem, gz_sem, act_sem, r_sem,
):
    me_c = lax.axis_index("ctx")
    me_g = lax.axis_index("grp")
    z, y = me_c // NY, me_c % NY
    x, zh, core = me_g // 4, (me_g // 2) % 2, me_g % 2
    me_q = x * 2 + core
    partner = {"grp": x * 4 + (1 - zh) * 2 + core}

    def near(d, c):
        return {"grp": ((x + d) % NX) * 4 + zh * 2 + c}

    pairs = (
        (prompt_hbm, prompt),
        (qn_hbm, qn),
        (w_uk_hbm, w_uk),
        (qr_hbm, qr),
        (w_uv_hbm, w_uv),
        (w_out_hbm, w_out),
        (wg_hbm, wgu.at[pl.ds(0, COLS), pl.ds(0, FF)]),
        (wu_hbm, wgu.at[pl.ds(0, COLS), pl.ds(FF, FF)]),
        (wd_hbm, wd),
    )
    loads = [pltpu.make_async_copy(a, b, load_sem.at[i]) for i, (a, b) in enumerate(pairs)]
    for load in loads[0:5]:
        load.start()
    barrier = pltpu.get_barrier_semaphore()
    sibling = near(0, 1 - core)
    others = [((z + dz) % NZ) * NY + (y + dy) % NY for dz, dy in OFFSETS]
    sources = [((z + NZ - dz) % NZ) * NY + (y + NY - dy) % NY for dz, dy in OFFSETS]
    greeted = [partner] + [{"ctx": c} for c in others]
    greeted += [near(d, c) for d in FAR_FIRST[:3] for c in range(2)] + [sibling]
    for device in greeted:
        pl.semaphore_signal(barrier, inc=1, device_id=device, device_id_type=MESH)
    sent = []

    def send(src, dst, sems, n, at, device):
        copy = pltpu.make_async_remote_copy(
            src_ref=src, dst_ref=dst, send_sem=sems.at[0, n], recv_sem=sems.at[1, at],
            device_id=device, device_id_type=MESH,
        )
        copy.start()
        sent.append((src, sems, n))

    def arrive(dst, sems, at):
        pltpu.make_async_remote_copy(
            src_ref=dst, dst_ref=dst, send_sem=sems.at[0, at], recv_sem=sems.at[1, at],
            device_id=partner, device_id_type=MESH,
        ).wait_recv()

    def spread(buf, sems):
        for d in (2, 1, 3):
            send(buf.at[me_q], buf.at[me_q], sems, d, d, near(d, core))
        send(buf.at[me_q], buf.at[me_q], sems, NX, NX, sibling)
        for d in (1, 3, 2):
            got = ((x + NX - d) % NX) * 2 + core
            arrive(buf.at[got], sems, d)
            send(buf.at[got], buf.at[got], sems, NX + d, NX + d, sibling)
        for d in (0, 1, 3, 2):
            arrive(buf.at[((x + NX - d) % NX) * 2 + 1 - core], sems, NX + d)

    scale = (NOPE + ROPE) ** -0.5
    loads[0].wait()
    keys[...] = prompt[...].T
    loads[1].wait()
    q_wide[...] = qn[...].astype(F32)
    for load in loads[2:5]:
        load.wait()
    for load in loads[5:9]:
        load.start()
    for h in range(HEADS):
        q = q_wide[pl.ds(h, ROWS, stride=HEADS), :].astype(BF16)
        queries = jnp.concatenate([dot(w_uk[h], q, 0, 1).astype(BF16), qr[h]], axis=0)
        s = dot(keys[...], queries, 1, 0) * scale
        top = jnp.max(s, axis=0, keepdims=True)
        raised = jnp.exp(s - top)
        total = jnp.sum(raised, axis=0, keepdims=True)
        weighted = dot(prompt[0:LAT, :], raised.astype(BF16), 1, 0)
        high, low = split(weighted)
        values = dot(w_uv[h], high, 0, 0) + dot(w_uv[h], low, 0, 0)
        o = (values / total).astype(BF16)
        obuf[h] = o.reshape(2, VDIM // 2, ROWS)
        lse[h] = jnp.broadcast_to(top + jnp.log(total), (8, ROWS))
    pl.semaphore_wait(barrier, len(greeted))
    for d in FAR_FIRST:
        h = (x + d) % NX
        for c in range(2) if d else (1 - core,):
            send(obuf.at[h, c], o_recv.at[d * 2 + core], o_sem, d * 2 + c, d * 2 + core, near(d, c))
            send(lse.at[h], l_recv.at[d * 2 + core], l_sem, d * 2 + c, d * 2 + core, near(d, c))
    o_recv[core] = obuf[x, core]
    l_recv[core] = lse[x]

    wgu[COLS:PAD, :] = jnp.zeros((PAD - COLS, 2 * FF), BF16)
    slot = lax.broadcasted_iota(jnp.int32, (PAD, PAD), 0)
    place = lax.broadcasted_iota(jnp.int32, (PAD, PAD), 1)

    def place_of(k):
        k2 = k % SLOTS
        return (k2 // CAP) * (QS * CAP) + (k // SLOTS) * CAP + k2 % CAP

    perm[...] = jnp.where(place_of(slot) == place, 1.0, 0.0).astype(BF16)
    perm_t[...] = jnp.where(place_of(place) == slot, 1.0, 0.0).astype(BF16)
    res_pad[...] = jnp.zeros((ROW_DEV, PAD), F32)
    res_pad[:, 0:COLS] = residual[...].astype(F32)
    proj[:, PAD - LANES : PAD] = jnp.zeros((ROWS, LANES), F32)
    down[:, PAD - LANES : PAD] = jnp.zeros((SLOTS, LANES), F32)

    lane = lax.broadcasted_iota(jnp.int32, (ROW_DEV, PAD), 1)
    expert_of = lane // (QS * CAP)
    scored = scores[...]
    gate_weights = ROUTE_FACTOR * scored / jnp.sum(scored, axis=1, keepdims=True)
    chosen = jnp.zeros((ROW_DEV, PAD), F32)
    weight = jnp.zeros((ROW_DEV, PAD), F32)
    for k in range(TOPK):
        hit = routes[:, k : k + 1] == expert_of
        chosen = chosen + jnp.where(hit, 1.0, 0.0)
        weight = weight + jnp.where(hit, gate_weights[:, k : k + 1], 0.0)
    row = lax.broadcasted_iota(jnp.int32, (ROW_DEV, PAD), 0)
    before = jnp.zeros((ROW_DEV, PAD), F32)
    for r in range(ROW_DEV - 1):
        before = before + jnp.where(row > r, chosen[r : r + 1, :], 0.0)
    picked = jnp.where(before == (lane % CAP).astype(F32), chosen, 0.0)
    block_of = (lane // CAP) % QS
    pick = jnp.concatenate([jnp.where(block_of == q, picked, 0.0) for q in range(QS)], axis=0)
    pick_weight = jnp.concatenate(
        [jnp.where(block_of == q, picked * weight, 0.0) for q in range(QS)], axis=0
    )

    loads[5].wait()
    w_out_t[...] = w_out[...].T

    for d in FAR_FIRST:
        for c in range(2) if d else (1 - core,):
            arrive(o_recv.at[d * 2 + c], o_sem, d * 2 + c)
            arrive(l_recv.at[d * 2 + c], l_sem, d * 2 + c)

    def merge(outs, sums):
        top = sums[0]
        for v in sums[1:]:
            top = jnp.maximum(top, v)
        scaled = [jnp.exp(v - top) for v in sums]
        total = scaled[0]
        for v in scaled[1:]:
            total = total + v
        o = jnp.zeros(outs[0].shape, F32)
        for v, s in zip(outs, scaled):
            o = o + v.astype(F32) * s
        return o / total, top + jnp.log(total)

    o, l = merge([o_recv[i] for i in range(2 * NX)], [l_recv[i, 0:1, :] for i in range(2 * NX)])
    zh_send[...] = o.astype(BF16)
    zl_send[...] = jnp.broadcast_to(l, (8, ROWS))
    send(zh_send, zh_recv, zh_sem, 0, 0, partner)
    send(zl_send, zl_recv, zh_sem, 1, 1, partner)
    loads[8].wait()
    wd_t[...] = wd[...].T
    arrive(zh_recv, zh_sem, 0)
    arrive(zl_recv, zh_sem, 1)
    o, _ = merge([zh_send[...], zh_recv[...]], [l, zl_recv[0:1, :]])
    att[me_q] = o.astype(BF16)
    spread(att, ag_sem)

    proj[:, 0:COLS] = dot(att[...].reshape(HEADS * VDIM, ROWS), w_out_t[...], 0, 0)
    for to in range(NY):
        parts = []
        for q in range(QS):
            part = proj[:, q * LANES : (q + 1) * LANES].reshape(NZ, NY, ROW_DEV, LANES)
            parts.append(part[:, to])
        pbuf[to] = jnp.stack(parts, axis=1).reshape(NZ * QS * ROW_DEV, LANES).astype(BF16)
    for d in (2, 1, 3):
        to = (y + d) % NY
        send(pbuf.at[to], p_recv.at[d], y_sem, d, d, {"ctx": z * NY + to})
    total = pbuf[y].astype(F32)
    for d in (1, 3, 2):
        arrive(p_recv.at[d], y_sem, d)
        total = total + p_recv[d].astype(F32)
    zbuf[...] = total.reshape(NZ, QS * ROW_DEV, LANES).astype(BF16)
    for d in (4, 3, 5, 2, 6, 1, 7):
        to = (z + d) % NZ
        send(zbuf.at[to], z_recv.at[d], z_sem, d, d, {"ctx": to * NY + y})
    hidden = jnp.concatenate([res_pad[:, q * LANES : (q + 1) * LANES] for q in range(QS)], axis=0)
    hidden = hidden + zbuf[z].astype(F32)
    for d in (1, 7, 2, 6, 3, 5, 4):
        arrive(z_recv.at[d], z_sem, d)
        hidden = hidden + z_recv[d].astype(F32)

    outgoing = dot(pick.astype(BF16), hidden.astype(BF16), 0, 0).astype(BF16)
    disp[...] = outgoing.reshape(NCTX, QS * CAP, LANES)
    def to_all(src, dst, sems):
        dst[me_c] = src[me_c]
        for n, to in enumerate(others):
            send(src.at[to], dst.at[me_c], sems, n, n, {"ctx": to})

    def from_all(dst, sems):
        for n, source in enumerate(sources):
            arrive(dst.at[source], sems, n)

    to_all(disp, arrived, d_sem)
    loads[6].wait()
    loads[7].wait()
    from_all(arrived, d_sem)
    rows = dot(perm[...], arrived[...].reshape(PAD, LANES), 1, 0).astype(BF16)
    rows = jnp.concatenate([rows[q * SLOTS : (q + 1) * SLOTS] for q in range(QS)], axis=1)

    wide = 2 * LANES
    for d in FAR_FIRST:
        first = pl.multiple_of(((x + d) % NX) * wide, wide)
        gate = dot(rows, wgu[:, pl.ds(first, wide)], 1, 0)
        up = dot(rows, wgu[:, pl.ds(FF + first, wide)], 1, 0)
        even = jnp.concatenate([gate[:, 0:LANES], up[:, 0:LANES]], axis=0)
        odd = jnp.concatenate([gate[:, LANES:wide], up[:, LANES:wide]], axis=0)
        gu_own[d] = jnp.where(core == 0, even, odd)
        gu_send[d] = jnp.where(core == 0, odd, even).astype(BF16)
        send(gu_send.at[d], gu_recv.at[d], gs_sem, d, d, sibling)
    for d in (2, 1, 3):
        arrive(gu_recv.at[d], gs_sem, d)
        gx_send[d] = (gu_own[d] + gu_recv[d].astype(F32)).astype(BF16)
        send(gx_send.at[d], gx_recv.at[d], g_sem, d, d, near(d, core))
    arrive(gu_recv.at[0], gs_sem, 0)
    sums = gu_own[0] + gu_recv[0].astype(F32)
    for d in (1, 3, 2):
        arrive(gx_recv.at[d], g_sem, d)
        sums = sums + gx_recv[d].astype(F32)
    gz_send[...] = sums.astype(BF16)
    send(gz_send, gz_recv, gz_sem, 0, 0, partner)
    arrive(gz_recv, gz_sem, 0)
    sums = sums + gz_recv[...].astype(F32)
    gate, up = sums[0:SLOTS], sums[SLOTS : 2 * SLOTS]
    act[me_q] = (gate / (1.0 + jnp.exp(-gate)) * up).astype(BF16)
    spread(act, act_sem)
    hidden_units = jnp.concatenate([act[q] for q in range(2 * NX)], axis=1)
    down[:, 0:COLS] = dot(hidden_units, wd_t[...], 1, 0)

    result = jnp.concatenate([down[:, q * LANES : (q + 1) * LANES] for q in range(QS)], axis=0)
    packed = dot(perm_t[...], result.astype(BF16), 1, 0).astype(BF16)
    ret[...] = packed.reshape(NCTX, QS * CAP, LANES)
    to_all(ret, ret_recv, r_sem)
    from_all(ret_recv, r_sem)
    returned = ret_recv[...].reshape(PAD, LANES)
    high, low = split(pick_weight)
    final = (hidden + dot(high, returned, 1, 0) + dot(low, returned, 1, 0)).astype(BF16)
    for q in range(QS):
        width = min(LANES, COLS - q * LANES)
        out[:, q * LANES : q * LANES + width] = final[q * ROW_DEV : (q + 1) * ROW_DEV, 0:width]

    for src, sems, n in sent:
        pltpu.make_async_remote_copy(
            src_ref=src, dst_ref=src, send_sem=sems.at[0, n], recv_sem=sems.at[1, n],
            device_id=partner, device_id_type=MESH,
        ).wait_send()


def per_device(
    q_nope, q_rope, w_uk, w_uv, prompt, w_out, residual, routes, route_scores,
    expert_gate, expert_up, expert_down,
):
    vmem, hbm = pl.BlockSpec(memory_space=pltpu.VMEM), pl.BlockSpec(memory_space=pl.ANY)
    dma = pltpu.SemaphoreType.DMA
    near = 2 * NX
    half = VDIM // 2
    scratch = [
        ((ROWS * HEADS, NOPE), BF16),
        ((ROWS * HEADS, NOPE), F32),
        ((HEADS, ROPE, ROWS), BF16),
        ((HEADS, NOPE, LAT), BF16),
        ((HEADS, LAT, VDIM), BF16),
        ((LAT + ROPE, KEYS), BF16),
        ((KEYS, LAT + ROPE), BF16),
        ((COLS, HEADS * VDIM), BF16),
        ((HEADS * VDIM, COLS), BF16),
        ((PAD, 2 * FF), BF16),
        ((COLS, FF), BF16),
        ((FF, COLS), BF16),
        ((PAD, PAD), BF16),
        ((PAD, PAD), BF16),
        ((HEADS, 2, half, ROWS), BF16),
        ((HEADS, 8, ROWS), F32),
        ((near, half, ROWS), BF16),
        ((near, 8, ROWS), F32),
        ((half, ROWS), BF16),
        ((half, ROWS), BF16),
        ((8, ROWS), F32),
        ((8, ROWS), F32),
        ((near, half, ROWS), BF16),
        ((ROWS, PAD), F32),
        ((NY, ROWS, LANES), BF16),
        ((NY, ROWS, LANES), BF16),
        ((NZ, QS * ROW_DEV, LANES), BF16),
        ((NZ, QS * ROW_DEV, LANES), BF16),
        ((ROW_DEV, PAD), F32),
        ((NCTX, QS * CAP, LANES), BF16),
        ((NCTX, QS * CAP, LANES), BF16),
        ((NX, 2 * SLOTS, LANES), F32),
        ((NX, 2 * SLOTS, LANES), BF16),
        ((NX, 2 * SLOTS, LANES), BF16),
        ((NX, 2 * SLOTS, LANES), BF16),
        ((NX, 2 * SLOTS, LANES), BF16),
        ((2 * SLOTS, LANES), BF16),
        ((2 * SLOTS, LANES), BF16),
        ((near, SLOTS, LANES), BF16),
        ((SLOTS, PAD), F32),
        ((NCTX, QS * CAP, LANES), BF16),
        ((NCTX, QS * CAP, LANES), BF16),
    ]
    sems = [(9,)] + [(2, n) for n in (near, near, 2, near, NY, NZ, NCTX, NX, NX, 1, near, NCTX)]
    return pl.pallas_call(
        kernel,
        out_shape=pltpu.VMEM((ROW_DEV, COLS), BF16),
        in_specs=[vmem] * 3 + [hbm] * 9,
        out_specs=vmem,
        scratch_shapes=[pltpu.VMEM(*s) for s in scratch] + [dma(s) for s in sems],
        compiler_params=pltpu.CompilerParams(
            collective_id=0, has_side_effects=True, vmem_limit_bytes=60 * 2**20
        ),
        name="layer",
    )(
        residual, routes, route_scores,
        q_nope.reshape(ROWS * HEADS, NOPE), jnp.transpose(q_rope, (1, 2, 0)), w_uk, w_uv, prompt.T,
        w_out.T, expert_gate[0], expert_up[0], expert_down[0].T,
    )


def solution(mesh):
    in_specs = (
        P(None, "ctx", None),
        P(None, "ctx", None),
        P("ctx", None, None),
        P("ctx", None, None),
        P("grp", None),
        P("ctx", "grp"),
        P("ctx", "grp"),
        P("ctx", None),
        P("ctx", None),
        P("ctx", "grp", None),
        P("ctx", "grp", None),
        P("ctx", None, "grp"),
    )
    return jax.shard_map(
        per_device, mesh=mesh, in_specs=in_specs, out_specs=P("ctx", "grp"), check_vma=False
    )
```

```python
import jax
import jax.numpy as jnp
from jax import lax
from jax.experimental import pallas as pl
from jax.experimental.pallas import tpu as pltpu
from jax.sharding import PartitionSpec as P

NOPE = 128
ROPE = 64
LAT = 512
VDIM = 128
CAP = 4
TOPK = 8
FF = 1024
ROWS = 256
HEADS = 4
KEYS = 384
COLS = 448
LANES = 128
PAD = 512
QS = PAD // LANES
ROW_DEV = 8
ROWS_Y = 64
NZ, NY, NX = 8, 4, 4
NCTX = NZ * NY
SLOTS = NCTX * CAP
ROUTE_FACTOR = 2.5
FAR_FIRST = (2, 1, 3, 0)
OFFSETS = [(dz, dy) for dz in (4, 3, 5, 2, 6, 1, 7, 0) for dy in FAR_FIRST][:-1]
F32 = jnp.float32
BF16 = jnp.bfloat16
MESH = pl.DeviceIdType.MESH


def dot(a, b, ca, cb):
    return lax.dot_general(a, b, (((ca,), (cb,)), ((), ())), preferred_element_type=F32)


def split(a):
    high = a.astype(BF16)
    return high, (a - high.astype(F32)).astype(BF16)


def kernel(
    residual, routes, scores,
    qn_hbm, qr_hbm, w_uk_hbm, w_uv_hbm, prompt_hbm, w_out_hbm, wg_hbm, wu_hbm, wd_hbm,
    out,
    qn, q_wide, qr, w_uk, w_uv, prompt, keys,
    w_out, w_out_t, wgu, wd, wd_t, perm, perm_t,
    obuf, lse, o_recv, l_recv, zh_send, zh_recv, zl_send, zl_recv, att_send, att,
    proj, zbuf, z_recv, res_pad, disp, arrived,
    gu_own, gu_send, gu_recv, gx_send, gx_recv, gz_send, gz_recv, act, down, ret, ret_recv,
    load_sem, o_sem, l_sem, zh_sem, ag_sem, w_sem, z_sem, d_sem, gs_sem, g_sem, gz_sem, act_sem, r_sem,
):
    me_c = lax.axis_index("ctx")
    me_g = lax.axis_index("grp")
    z, y = me_c // NY, me_c % NY
    x, zh, core = me_g // 4, (me_g // 2) % 2, me_g % 2
    me_q = x * 2 + core
    partner = {"grp": x * 4 + (1 - zh) * 2 + core}

    def near(d, c):
        return {"grp": ((x + d) % NX) * 4 + zh * 2 + c}

    pairs = (
        (prompt_hbm, prompt),
        (qn_hbm, qn),
        (w_uk_hbm, w_uk),
        (qr_hbm, qr),
        (w_uv_hbm, w_uv),
        (w_out_hbm, w_out.at[y]),
        (wg_hbm, wgu.at[pl.ds(0, COLS), pl.ds(0, FF)]),
        (wu_hbm, wgu.at[pl.ds(0, COLS), pl.ds(FF, FF)]),
        (wd_hbm, wd),
    )
    loads = [pltpu.make_async_copy(a, b, load_sem.at[i]) for i, (a, b) in enumerate(pairs)]
    for load in loads[0:5]:
        load.start()
    barrier = pltpu.get_barrier_semaphore()
    sibling = near(0, 1 - core)

    def across(dx, dy):
        return {
            "ctx": z * NY + (y + dy) % NY,
            "grp": ((x + dx) % NX) * 4 + zh * 2 + core,
        }

    others = [((z + dz) % NZ) * NY + (y + dy) % NY for dz, dy in OFFSETS]
    sources = [((z + NZ - dz) % NZ) * NY + (y + NY - dy) % NY for dz, dy in OFFSETS]
    greeted = [partner] + [{"ctx": c} for c in others]
    greeted += [across(dx, dy) for dx in (2, 1, 3) for dy in (2, 1, 3)]
    greeted += [near(d, c) for d in FAR_FIRST[:3] for c in range(2)] + [sibling]
    for device in greeted:
        pl.semaphore_signal(barrier, inc=1, device_id=device, device_id_type=MESH)
    sent = []

    def send(src, dst, sems, n, at, device):
        copy = pltpu.make_async_remote_copy(
            src_ref=src, dst_ref=dst, send_sem=sems.at[0, n], recv_sem=sems.at[1, at],
            device_id=device, device_id_type=MESH,
        )
        copy.start()
        sent.append((src, sems, n))

    def arrive(dst, sems, at):
        pltpu.make_async_remote_copy(
            src_ref=dst, dst_ref=dst, send_sem=sems.at[0, at], recv_sem=sems.at[1, at],
            device_id=partner, device_id_type=MESH,
        ).wait_recv()

    def spread(buf, sems):
        for d in (2, 1, 3):
            send(buf.at[me_q], buf.at[me_q], sems, d, d, near(d, core))
        send(buf.at[me_q], buf.at[me_q], sems, NX, NX, sibling)
        for d in (1, 3, 2):
            got = ((x + NX - d) % NX) * 2 + core
            arrive(buf.at[got], sems, d)
            send(buf.at[got], buf.at[got], sems, NX + d, NX + d, sibling)
        for d in (0, 1, 3, 2):
            arrive(buf.at[((x + NX - d) % NX) * 2 + 1 - core], sems, NX + d)

    scale = (NOPE + ROPE) ** -0.5
    loads[0].wait()
    keys[...] = prompt[...].T
    loads[1].wait()
    q_wide[...] = qn[...].astype(F32)
    for load in loads[2:5]:
        load.wait()
    given = lax.broadcasted_iota(jnp.int32, (ROWS, ROWS), 0)
    wanted = lax.broadcasted_iota(jnp.int32, (ROWS, ROWS), 1)
    wanted = (
        (wanted % ROWS_Y) // ROW_DEV * (NY * ROW_DEV)
        + wanted // ROWS_Y * ROW_DEV
        + wanted % ROW_DEV
    )
    order = jnp.where(given == wanted, 1.0, 0.0).astype(BF16)
    rotated = dot(qr[...].reshape(HEADS * ROPE, ROWS), order, 1, 0).astype(BF16)
    for load in loads[5:9]:
        load.start()
    for h in range(HEADS):
        q = [
            q_wide[pl.ds((zz * NY + yy) * ROW_DEV * HEADS + h, ROW_DEV, stride=HEADS), :]
            for yy in range(NY)
            for zz in range(NZ)
        ]
        q = jnp.concatenate(q, axis=0).astype(BF16)
        queries = jnp.concatenate([dot(w_uk[h], q, 0, 1).astype(BF16), rotated[h * ROPE : (h + 1) * ROPE]], axis=0)
        s = dot(keys[...], queries, 1, 0) * scale
        top = jnp.max(s, axis=0, keepdims=True)
        raised = jnp.exp(s - top)
        total = jnp.sum(raised, axis=0, keepdims=True)
        weighted = dot(prompt[0:LAT, :], raised.astype(BF16), 1, 0)
        high, low = split(weighted)
        values = dot(w_uv[h], high, 0, 0) + dot(w_uv[h], low, 0, 0)
        o = (values / total).astype(BF16)
        obuf[h] = o.reshape(2, VDIM // 2, ROWS)
        lse[h] = jnp.broadcast_to(top + jnp.log(total), (8, ROWS))
    pl.semaphore_wait(barrier, len(greeted))
    for d in FAR_FIRST:
        h = (x + d) % NX
        for c in range(2) if d else (1 - core,):
            send(obuf.at[h, c], o_recv.at[d * 2 + core], o_sem, d * 2 + c, d * 2 + core, near(d, c))
            send(lse.at[h], l_recv.at[d * 2 + core], l_sem, d * 2 + c, d * 2 + core, near(d, c))
    o_recv[core] = obuf[x, core]
    l_recv[core] = lse[x]

    wgu[COLS:PAD, :] = jnp.zeros((PAD - COLS, 2 * FF), BF16)
    slot = lax.broadcasted_iota(jnp.int32, (PAD, PAD), 0)
    place = lax.broadcasted_iota(jnp.int32, (PAD, PAD), 1)

    def place_of(k):
        k2 = k % SLOTS
        return (k2 // CAP) * (QS * CAP) + (k // SLOTS) * CAP + k2 % CAP

    perm[...] = jnp.where(place_of(slot) == place, 1.0, 0.0).astype(BF16)
    perm_t[...] = jnp.where(place_of(place) == slot, 1.0, 0.0).astype(BF16)
    res_pad[...] = jnp.zeros((ROW_DEV, PAD), F32)
    res_pad[:, 0:COLS] = residual[...].astype(F32)
    proj[:, PAD - LANES : PAD] = jnp.zeros((ROWS_Y, LANES), F32)
    down[:, PAD - LANES : PAD] = jnp.zeros((SLOTS, LANES), F32)

    lane = lax.broadcasted_iota(jnp.int32, (ROW_DEV, PAD), 1)
    expert_of = lane // (QS * CAP)
    scored = scores[...]
    gate_weights = ROUTE_FACTOR * scored / jnp.sum(scored, axis=1, keepdims=True)
    chosen = jnp.zeros((ROW_DEV, PAD), F32)
    weight = jnp.zeros((ROW_DEV, PAD), F32)
    for k in range(TOPK):
        hit = routes[:, k : k + 1] == expert_of
        chosen = chosen + jnp.where(hit, 1.0, 0.0)
        weight = weight + jnp.where(hit, gate_weights[:, k : k + 1], 0.0)
    row = lax.broadcasted_iota(jnp.int32, (ROW_DEV, PAD), 0)
    before = jnp.zeros((ROW_DEV, PAD), F32)
    for r in range(ROW_DEV - 1):
        before = before + jnp.where(row > r, chosen[r : r + 1, :], 0.0)
    picked = jnp.where(before == (lane % CAP).astype(F32), chosen, 0.0)
    block_of = (lane // CAP) % QS
    pick = jnp.concatenate([jnp.where(block_of == q, picked, 0.0) for q in range(QS)], axis=0)
    pick_weight = jnp.concatenate(
        [jnp.where(block_of == q, picked * weight, 0.0) for q in range(QS)], axis=0
    )

    loads[5].wait()
    for d in (2, 1, 3):
        send(w_out.at[y], w_out.at[y], w_sem, d, d, {"ctx": z * NY + (y + d) % NY})

    for d in FAR_FIRST:
        for c in range(2) if d else (1 - core,):
            arrive(o_recv.at[d * 2 + c], o_sem, d * 2 + c)
            arrive(l_recv.at[d * 2 + c], l_sem, d * 2 + c)

    def merge(outs, sums):
        top = sums[0]
        for v in sums[1:]:
            top = jnp.maximum(top, v)
        scaled = [jnp.exp(v - top) for v in sums]
        total = scaled[0]
        for v in scaled[1:]:
            total = total + v
        o = jnp.zeros(outs[0].shape, F32)
        for v, s in zip(outs, scaled):
            o = o + v.astype(F32) * s
        return o / total, top + jnp.log(total)

    o, l = merge([o_recv[i] for i in range(2 * NX)], [l_recv[i, 0:1, :] for i in range(2 * NX)])
    zh_send[...] = o.astype(BF16)
    zl_send[...] = jnp.broadcast_to(l, (8, ROWS))
    send(zh_send, zh_recv, zh_sem, 0, 0, partner)
    send(zl_send, zl_recv, zh_sem, 1, 1, partner)
    loads[8].wait()
    wd_t[...] = wd[...].T
    for d in (1, 3, 2):
        arrive(w_out.at[(y + NY - d) % NY], w_sem, d)
    for yy in range(NY):
        turned = w_out[yy].T
        for xx in range(NX):
            for c in range(2):
                for half in range(2):
                    first = (xx * 2 + c) * 64 + half * 32
                    w_out_t[half, c, yy, xx] = turned[first : first + 32]
    arrive(zh_recv, zh_sem, 0)
    arrive(zl_recv, zh_sem, 1)
    o, _ = merge([zh_send[...], zh_recv[...]], [l, zl_recv[0:1, :]])
    left = lax.broadcasted_iota(jnp.int32, (32, LANES), 1) < 64
    for t in range(2):
        a, b = o[0:32, t * LANES : (t + 1) * LANES], o[32:64, t * LANES : (t + 1) * LANES]
        att_send[2 * t] = jnp.where(left, a, pltpu.roll(b, 64, 1)).astype(BF16)
        att_send[2 * t + 1] = jnp.where(left, pltpu.roll(a, 64, 1), b).astype(BF16)
    steps = [(dx, dy) for dx in FAR_FIRST for dy in FAR_FIRST][:-1]
    for n, (dx, dy) in enumerate(steps):
        send(att_send.at[(y + dy) % NY], att.at[core, y, x], ag_sem, n, n, across(dx, dy))
    att[core, y, x] = att_send[y]
    for n, (dx, dy) in enumerate(steps):
        arrive(att.at[core, (y + NY - dy) % NY, (x + NX - dx) % NX], ag_sem, n)
    send(att.at[core], att.at[core], ag_sem, len(steps), len(steps), sibling)
    arrive(att.at[1 - core], ag_sem, len(steps))

    depth = 2 * NY * NX * 32
    packed = att[...].reshape(depth, LANES)
    proj[:, 0:COLS] = (
        dot(packed, w_out_t[0].reshape(depth, COLS), 0, 0)[0:ROWS_Y]
        + dot(packed, w_out_t[1].reshape(depth, COLS), 0, 0)[ROWS_Y : 2 * ROWS_Y]
    )
    parts = [
        proj[:, q * LANES : (q + 1) * LANES].reshape(NZ, ROW_DEV, LANES) for q in range(QS)
    ]
    zbuf[...] = jnp.stack(parts, axis=1).reshape(NZ, QS * ROW_DEV, LANES).astype(BF16)
    for d in (4, 3, 5, 2, 6, 1, 7):
        to = (z + d) % NZ
        send(zbuf.at[to], z_recv.at[d], z_sem, d, d, {"ctx": to * NY + y})
    hidden = jnp.concatenate([res_pad[:, q * LANES : (q + 1) * LANES] for q in range(QS)], axis=0)
    hidden = hidden + zbuf[z].astype(F32)
    for d in (1, 7, 2, 6, 3, 5, 4):
        arrive(z_recv.at[d], z_sem, d)
        hidden = hidden + z_recv[d].astype(F32)

    outgoing = dot(pick.astype(BF16), hidden.astype(BF16), 0, 0).astype(BF16)
    disp[...] = outgoing.reshape(NCTX, QS * CAP, LANES)
    def to_all(src, dst, sems):
        dst[me_c] = src[me_c]
        for n, to in enumerate(others):
            send(src.at[to], dst.at[me_c], sems, n, n, {"ctx": to})

    def from_all(dst, sems):
        for n, source in enumerate(sources):
            arrive(dst.at[source], sems, n)

    to_all(disp, arrived, d_sem)
    loads[6].wait()
    loads[7].wait()
    from_all(arrived, d_sem)
    rows = dot(perm[...], arrived[...].reshape(PAD, LANES), 1, 0).astype(BF16)
    rows = jnp.concatenate([rows[q * SLOTS : (q + 1) * SLOTS] for q in range(QS)], axis=1)

    wide = 2 * LANES
    for d in FAR_FIRST:
        first = pl.multiple_of(((x + d) % NX) * wide, wide)
        gate = dot(rows, wgu[:, pl.ds(first, wide)], 1, 0)
        up = dot(rows, wgu[:, pl.ds(FF + first, wide)], 1, 0)
        even = jnp.concatenate([gate[:, 0:LANES], up[:, 0:LANES]], axis=0)
        odd = jnp.concatenate([gate[:, LANES:wide], up[:, LANES:wide]], axis=0)
        gu_own[d] = jnp.where(core == 0, even, odd)
        gu_send[d] = jnp.where(core == 0, odd, even).astype(BF16)
        send(gu_send.at[d], gu_recv.at[d], gs_sem, d, d, sibling)
    for d in (2, 1, 3):
        arrive(gu_recv.at[d], gs_sem, d)
        gx_send[d] = (gu_own[d] + gu_recv[d].astype(F32)).astype(BF16)
        send(gx_send.at[d], gx_recv.at[d], g_sem, d, d, near(d, core))
    arrive(gu_recv.at[0], gs_sem, 0)
    sums = gu_own[0] + gu_recv[0].astype(F32)
    for d in (1, 3, 2):
        arrive(gx_recv.at[d], g_sem, d)
        sums = sums + gx_recv[d].astype(F32)
    gz_send[...] = sums.astype(BF16)
    send(gz_send, gz_recv, gz_sem, 0, 0, partner)
    arrive(gz_recv, gz_sem, 0)
    sums = sums + gz_recv[...].astype(F32)
    gate, up = sums[0:SLOTS], sums[SLOTS : 2 * SLOTS]
    act[me_q] = (gate / (1.0 + jnp.exp(-gate)) * up).astype(BF16)
    spread(act, act_sem)
    hidden_units = jnp.concatenate([act[q] for q in range(2 * NX)], axis=1)
    down[:, 0:COLS] = dot(hidden_units, wd_t[...], 1, 0)

    result = jnp.concatenate([down[:, q * LANES : (q + 1) * LANES] for q in range(QS)], axis=0)
    packed = dot(perm_t[...], result.astype(BF16), 1, 0).astype(BF16)
    ret[...] = packed.reshape(NCTX, QS * CAP, LANES)
    to_all(ret, ret_recv, r_sem)
    from_all(ret_recv, r_sem)
    returned = ret_recv[...].reshape(PAD, LANES)
    high, low = split(pick_weight)
    final = (hidden + dot(high, returned, 1, 0) + dot(low, returned, 1, 0)).astype(BF16)
    for q in range(QS):
        width = min(LANES, COLS - q * LANES)
        out[:, q * LANES : q * LANES + width] = final[q * ROW_DEV : (q + 1) * ROW_DEV, 0:width]

    for src, sems, n in sent:
        pltpu.make_async_remote_copy(
            src_ref=src, dst_ref=src, send_sem=sems.at[0, n], recv_sem=sems.at[1, n],
            device_id=partner, device_id_type=MESH,
        ).wait_send()


def per_device(
    q_nope, q_rope, w_uk, w_uv, prompt, w_out, residual, routes, route_scores,
    expert_gate, expert_up, expert_down,
):
    vmem, hbm = pl.BlockSpec(memory_space=pltpu.VMEM), pl.BlockSpec(memory_space=pl.ANY)
    dma = pltpu.SemaphoreType.DMA
    near = 2 * NX
    half = VDIM // 2
    scratch = [
        ((ROWS * HEADS, NOPE), BF16),
        ((ROWS * HEADS, NOPE), F32),
        ((HEADS, ROPE, ROWS), BF16),
        ((HEADS, NOPE, LAT), BF16),
        ((HEADS, LAT, VDIM), BF16),
        ((LAT + ROPE, KEYS), BF16),
        ((KEYS, LAT + ROPE), BF16),
        ((NY, COLS, HEADS * VDIM), BF16),
        ((2, 2, NY, NX, 32, COLS), BF16),
        ((PAD, 2 * FF), BF16),
        ((COLS, FF), BF16),
        ((FF, COLS), BF16),
        ((PAD, PAD), BF16),
        ((PAD, PAD), BF16),
        ((HEADS, 2, half, ROWS), BF16),
        ((HEADS, 8, ROWS), F32),
        ((near, half, ROWS), BF16),
        ((near, 8, ROWS), F32),
        ((half, ROWS), BF16),
        ((half, ROWS), BF16),
        ((8, ROWS), F32),
        ((8, ROWS), F32),
        ((NY, 32, LANES), BF16),
        ((2, NY, NX, 32, LANES), BF16),
        ((ROWS_Y, PAD), F32),
        ((NZ, QS * ROW_DEV, LANES), BF16),
        ((NZ, QS * ROW_DEV, LANES), BF16),
        ((ROW_DEV, PAD), F32),
        ((NCTX, QS * CAP, LANES), BF16),
        ((NCTX, QS * CAP, LANES), BF16),
        ((NX, 2 * SLOTS, LANES), F32),
        ((NX, 2 * SLOTS, LANES), BF16),
        ((NX, 2 * SLOTS, LANES), BF16),
        ((NX, 2 * SLOTS, LANES), BF16),
        ((NX, 2 * SLOTS, LANES), BF16),
        ((2 * SLOTS, LANES), BF16),
        ((2 * SLOTS, LANES), BF16),
        ((near, SLOTS, LANES), BF16),
        ((SLOTS, PAD), F32),
        ((NCTX, QS * CAP, LANES), BF16),
        ((NCTX, QS * CAP, LANES), BF16),
    ]
    sems = [(9,)] + [(2, n) for n in (near, near, 2, NX * NY, NY, NZ, NCTX, NX, NX, 1, near, NCTX)]
    return pl.pallas_call(
        kernel,
        out_shape=pltpu.VMEM((ROW_DEV, COLS), BF16),
        in_specs=[vmem] * 3 + [hbm] * 9,
        out_specs=vmem,
        scratch_shapes=[pltpu.VMEM(*s) for s in scratch] + [dma(s) for s in sems],
        compiler_params=pltpu.CompilerParams(
            collective_id=0, has_side_effects=True, vmem_limit_bytes=60 * 2**20
        ),
        name="layer",
    )(
        residual, routes, route_scores,
        q_nope.reshape(ROWS * HEADS, NOPE), jnp.transpose(q_rope, (1, 2, 0)), w_uk, w_uv, prompt.T,
        w_out.T, expert_gate[0], expert_up[0], expert_down[0].T,
    )


def solution(mesh):
    in_specs = (
        P(None, "ctx", None),
        P(None, "ctx", None),
        P("ctx", None, None),
        P("ctx", None, None),
        P("grp", None),
        P("ctx", "grp"),
        P("ctx", "grp"),
        P("ctx", None),
        P("ctx", None),
        P("ctx", "grp", None),
        P("ctx", "grp", None),
        P("ctx", None, "grp"),
    )
    return jax.shard_map(
        per_device, mesh=mesh, in_specs=in_specs, out_specs=P("ctx", "grp"), check_vma=False
    )
```

```python
import jax
import jax.numpy as jnp
from jax import lax
from jax.experimental import pallas as pl
from jax.experimental.pallas import tpu as pltpu
from jax.sharding import PartitionSpec as P

NOPE = 128
ROPE = 64
LAT = 512
VDIM = 128
CAP = 4
TOPK = 8
FF = 1024
ROWS = 256
HEADS = 4
KEYS = 384
COLS = 448
LANES = 128
PAD = 512
QS = PAD // LANES
ROW_DEV = 8
HALF_Z = 4
NZ, NY, NX = 8, 4, 4
NCTX = NZ * NY
SLOTS = NCTX * CAP
ROUTE_FACTOR = 2.5
FAR_FIRST = (2, 1, 3, 0)
OFFSETS = [(dz, dy) for dz in (4, 3, 5, 2, 6, 1, 7, 0) for dy in FAR_FIRST][:-1]
F32 = jnp.float32
BF16 = jnp.bfloat16
MESH = pl.DeviceIdType.MESH


def dot(a, b, ca, cb):
    return lax.dot_general(a, b, (((ca,), (cb,)), ((), ())), preferred_element_type=F32)


def split(a):
    high = a.astype(BF16)
    return high, (a - high.astype(F32)).astype(BF16)


def kernel(
    residual_hbm, routes_hbm, scores_hbm,
    qn_hbm, qr_hbm, w_uk_hbm, w_uv_hbm, prompt_hbm, w_out_hbm, wg_hbm, wu_hbm, wd_hbm,
    out,
    residual, routes, scores,
    qn, q_wide, qr, w_uk, w_uv, prompt, keys,
    w_out, w_out_t, wgu, wd, wd_t, perm, perm_t,
    obuf, lse, o_recv, l_recv, zh_send, zh_recv, zl_send, zl_recv, att,
    proj, pbuf, p_recv, zbuf, z_recv, res_pad, disp, arrived,
    gu_own, gu_send, gu_recv, gx_send, gx_recv, gz_send, gz_recv, act, down, ret, ret_recv,
    load_sem, o_sem, l_sem, zh_sem, ag_sem, y_sem, z_sem, d_sem, gs_sem, g_sem, gz_sem, act_sem, r_sem,
):
    me_c = lax.axis_index("ctx")
    me_g = lax.axis_index("grp")
    z, y = me_c // NY, me_c % NY
    x, zh, core = me_g // 4, (me_g // 2) % 2, me_g % 2
    me_q = x * 2 + core
    partner = {"grp": x * 4 + (1 - zh) * 2 + core}

    def near(d, c):
        return {"grp": ((x + d) % NX) * 4 + zh * 2 + c}

    barrier = pltpu.get_barrier_semaphore()
    sibling = near(0, 1 - core)
    others = [((z + dz) % NZ) * NY + (y + dy) % NY for dz, dy in OFFSETS]
    sources = [((z + NZ - dz) % NZ) * NY + (y + NY - dy) % NY for dz, dy in OFFSETS]
    greeted = [partner] + [{"ctx": c} for c in others]
    greeted += [near(d, c) for d in FAR_FIRST[:3] for c in range(2)] + [sibling]
    for device in greeted:
        pl.semaphore_signal(barrier, inc=1, device_id=device, device_id_type=MESH)
    pairs = (
        (prompt_hbm, prompt),
        (qn_hbm, qn),
        (w_uk_hbm, w_uk),
        (qr_hbm, qr),
        (w_uv_hbm, w_uv),
        (w_out_hbm, w_out),
        (wg_hbm, wgu.at[pl.ds(0, COLS), pl.ds(0, FF)]),
        (wu_hbm, wgu.at[pl.ds(0, COLS), pl.ds(FF, FF)]),
        (wd_hbm, wd),
        (residual_hbm, residual),
        (routes_hbm, routes),
        (scores_hbm, scores),
    )
    loads = [pltpu.make_async_copy(a, b, load_sem.at[i]) for i, (a, b) in enumerate(pairs)]
    for load in loads[0:5]:
        load.start()
    sent = []

    def send(src, dst, sems, n, at, device):
        copy = pltpu.make_async_remote_copy(
            src_ref=src, dst_ref=dst, send_sem=sems.at[0, n], recv_sem=sems.at[1, at],
            device_id=device, device_id_type=MESH,
        )
        copy.start()
        sent.append((src, sems, n))

    def arrive(dst, sems, at):
        pltpu.make_async_remote_copy(
            src_ref=dst, dst_ref=dst, send_sem=sems.at[0, at], recv_sem=sems.at[1, at],
            device_id=partner, device_id_type=MESH,
        ).wait_recv()

    def spread(buf, sems, use=lambda total, q: total, total=0):
        for d in (2, 1, 3):
            send(buf.at[me_q], buf.at[me_q], sems, d, d, near(d, core))
        send(buf.at[me_q], buf.at[me_q], sems, NX, NX, sibling)
        for d in (1, 3, 2):
            got = ((x + NX - d) % NX) * 2 + core
            arrive(buf.at[got], sems, d)
            send(buf.at[got], buf.at[got], sems, NX + d, NX + d, sibling)
        for d in (0, 1, 3, 2):
            total = use(total, ((x + NX - d) % NX) * 2 + core)
        for d in (0, 1, 3, 2):
            got = ((x + NX - d) % NX) * 2 + 1 - core
            arrive(buf.at[got], sems, NX + d)
            total = use(total, got)
        return total

    def fold(v):
        return jnp.concatenate([v[:, 0:LANES], v[:, LANES:ROWS]] * 4, axis=0)

    def unfold(v):
        return jnp.concatenate([v[0:1], v[1:2]], axis=1)

    scale = (NOPE + ROPE) ** -0.5
    loads[0].wait()
    keys[...] = prompt[...].T
    loads[1].wait()
    q_wide[...] = qn[...].astype(F32)
    for load in loads[2:5]:
        load.wait()
    for load in loads[5:12]:
        load.start()
    for h in range(HEADS):
        q = q_wide[pl.ds(h, ROWS, stride=HEADS), :].astype(BF16)
        queries = jnp.concatenate([dot(w_uk[h], q, 0, 1).astype(BF16), qr[h]], axis=0)
        s = dot(keys[...], queries, 1, 0) * scale
        top = jnp.max(s, axis=0, keepdims=True)
        raised = jnp.exp(s - top)
        total = jnp.sum(raised, axis=0, keepdims=True)
        weighted = dot(prompt[0:LAT, :], raised.astype(BF16), 1, 0)
        high, low = split(weighted)
        values = dot(w_uv[h], high, 0, 0) + dot(w_uv[h], low, 0, 0)
        o = (values / total).astype(BF16)
        obuf[h] = o.reshape(2, VDIM // 2, ROWS)
        lse[h] = fold(top + jnp.log(total))
    pl.semaphore_wait(barrier, len(greeted))
    for d in FAR_FIRST:
        h = (x + d) % NX
        for c in range(2) if d else (1 - core,):
            send(obuf.at[h, c], o_recv.at[d * 2 + core], o_sem, d * 2 + c, d * 2 + core, near(d, c))
            send(lse.at[h], l_recv.at[d * 2 + core], l_sem, d * 2 + c, d * 2 + core, near(d, c))
    o_recv[core] = obuf[x, core]
    l_recv[core] = lse[x]

    wgu[COLS:PAD, :] = jnp.zeros((PAD - COLS, 2 * FF), BF16)
    slot = lax.broadcasted_iota(jnp.int32, (PAD, PAD), 0)
    place = lax.broadcasted_iota(jnp.int32, (PAD, PAD), 1)

    def place_of(k):
        k2 = k % SLOTS
        return (k2 // CAP) * (QS * CAP) + (k // SLOTS) * CAP + k2 % CAP

    perm[...] = jnp.where(place_of(slot) == place, 1.0, 0.0).astype(BF16)
    perm_t[...] = jnp.where(place_of(place) == slot, 1.0, 0.0).astype(BF16)
    for load in loads[9:12]:
        load.wait()
    res_pad[...] = jnp.zeros((ROW_DEV, PAD), F32)
    res_pad[:, 0:COLS] = residual[...].astype(F32)
    proj[:, PAD - LANES : PAD] = jnp.zeros((ROWS, LANES), F32)
    down[:, PAD - LANES : PAD] = jnp.zeros((SLOTS, LANES), F32)

    lane = lax.broadcasted_iota(jnp.int32, (ROW_DEV, PAD), 1)
    expert_of = lane // (QS * CAP)
    scored = scores[...]
    gate_weights = ROUTE_FACTOR * scored / jnp.sum(scored, axis=1, keepdims=True)
    chosen = jnp.zeros((ROW_DEV, PAD), F32)
    weight = jnp.zeros((ROW_DEV, PAD), F32)
    for k in range(TOPK):
        hit = routes[:, k : k + 1] == expert_of
        chosen = chosen + jnp.where(hit, 1.0, 0.0)
        weight = weight + jnp.where(hit, gate_weights[:, k : k + 1], 0.0)
    row = lax.broadcasted_iota(jnp.int32, (ROW_DEV, PAD), 0)
    before = jnp.zeros((ROW_DEV, PAD), F32)
    for r in range(ROW_DEV - 1):
        before = before + jnp.where(row > r, chosen[r : r + 1, :], 0.0)
    picked = jnp.where(before == (lane % CAP).astype(F32), chosen, 0.0)
    block_of = (lane // CAP) % QS
    pick = jnp.concatenate([jnp.where(block_of == q, picked, 0.0) for q in range(QS)], axis=0)
    pick_weight = jnp.concatenate(
        [jnp.where(block_of == q, picked * weight, 0.0) for q in range(QS)], axis=0
    )

    loads[5].wait()
    w_out_t[...] = w_out[...].T

    for d in FAR_FIRST:
        for c in range(2) if d else (1 - core,):
            arrive(o_recv.at[d * 2 + c], o_sem, d * 2 + c)
            arrive(l_recv.at[d * 2 + c], l_sem, d * 2 + c)

    def merge(outs, sums):
        top = sums[0]
        for v in sums[1:]:
            top = jnp.maximum(top, v)
        scaled = [jnp.exp(v - top) for v in sums]
        total = scaled[0]
        for v in scaled[1:]:
            total = total + v
        o = jnp.zeros(outs[0].shape, F32)
        for v, s in zip(outs, scaled):
            o = o + v.astype(F32) * s
        return o / total, top + jnp.log(total)

    o, l = merge([o_recv[i] for i in range(2 * NX)], [unfold(l_recv[i]) for i in range(2 * NX)])
    zh_send[...] = o.astype(BF16)
    zl_send[...] = fold(l)
    send(zh_send, zh_recv, zh_sem, 0, 0, partner)
    send(zl_send, zl_recv, zh_sem, 1, 1, partner)
    loads[8].wait()
    wd_t[...] = wd[...].T
    arrive(zh_recv, zh_sem, 0)
    arrive(zl_recv, zh_sem, 1)
    o, _ = merge([zh_send[...], zh_recv[...]], [l, unfold(zl_recv[...])])
    att[me_q] = o.astype(BF16)
    spread(att, ag_sem)

    proj[:, 0:COLS] = dot(att[...].reshape(HEADS * VDIM, ROWS), w_out_t[...], 0, 0)
    for to in range(NY):
        parts = []
        for q in range(QS):
            part = proj[:, q * LANES : (q + 1) * LANES].reshape(NZ, NY, ROW_DEV, LANES)
            parts.append(part[:, to])
        block = jnp.stack(parts, axis=1).reshape(2, HALF_Z * QS * ROW_DEV, LANES)
        pbuf[to] = block.astype(BF16)
    halves = (1 - z // HALF_Z, z // HALF_Z)
    for k, half in enumerate(halves):
        for d in (2, 1, 3):
            to = (y + d) % NY
            device = {"ctx": z * NY + to}
            send(pbuf.at[to, half], p_recv.at[d, k], y_sem, d * 2 + k, d * 2 + k, device)
    for k, half in enumerate(halves):
        total = pbuf[y, half].astype(F32)
        for d in (1, 3, 2):
            arrive(p_recv.at[d, k], y_sem, d * 2 + k)
            total = total + p_recv[d, k].astype(F32)
        zbuf[half] = total.reshape(HALF_Z, QS * ROW_DEV, LANES).astype(BF16)
        for j in range(HALF_Z)[k:]:
            at = (z + j) % HALF_Z
            device = {"ctx": (half * HALF_Z + at) * NY + y}
            n = j + HALF_Z * (1 - k)
            send(zbuf.at[half, at], z_recv.at[n], z_sem, n, n, device)
    hidden = jnp.concatenate([res_pad[:, q * LANES : (q + 1) * LANES] for q in range(QS)], axis=0)
    hidden = hidden + zbuf[halves[1], z % HALF_Z].astype(F32)
    for d in range(1, NZ):
        arrive(z_recv.at[d], z_sem, d)
        hidden = hidden + z_recv[d].astype(F32)

    outgoing = dot(pick.astype(BF16), hidden.astype(BF16), 0, 0).astype(BF16)
    disp[...] = outgoing.reshape(NCTX, QS * CAP, LANES)
    def to_all(src, dst, sems):
        dst[me_c] = src[me_c]
        for n, to in enumerate(others):
            send(src.at[to], dst.at[me_c], sems, n, n, {"ctx": to})

    def from_all(dst, sems):
        for n, source in enumerate(sources):
            arrive(dst.at[source], sems, n)

    to_all(disp, arrived, d_sem)
    loads[6].wait()
    loads[7].wait()
    from_all(arrived, d_sem)
    rows = dot(perm[...], arrived[...].reshape(PAD, LANES), 1, 0).astype(BF16)
    rows = jnp.concatenate([rows[q * SLOTS : (q + 1) * SLOTS] for q in range(QS)], axis=1)

    wide = 2 * LANES
    for d in FAR_FIRST:
        first = pl.multiple_of(((x + d) % NX) * wide, wide)
        gate = dot(rows, wgu[:, pl.ds(first, wide)], 1, 0)
        up = dot(rows, wgu[:, pl.ds(FF + first, wide)], 1, 0)
        even = jnp.concatenate([gate[:, 0:LANES], up[:, 0:LANES]], axis=0)
        odd = jnp.concatenate([gate[:, LANES:wide], up[:, LANES:wide]], axis=0)
        gu_own[d] = jnp.where(core == 0, even, odd)
        gu_send[d] = jnp.where(core == 0, odd, even).astype(BF16)
        send(gu_send.at[d], gu_recv.at[d], gs_sem, d, d, sibling)
    for d in (2, 1, 3):
        arrive(gu_recv.at[d], gs_sem, d)
        gx_send[d] = (gu_own[d] + gu_recv[d].astype(F32)).astype(BF16)
        send(gx_send.at[d], gx_recv.at[d], g_sem, d, d, near(d, core))
    arrive(gu_recv.at[0], gs_sem, 0)
    sums = gu_own[0] + gu_recv[0].astype(F32)
    for d in (1, 3, 2):
        arrive(gx_recv.at[d], g_sem, d)
        sums = sums + gx_recv[d].astype(F32)
    gz_send[...] = sums.astype(BF16)
    send(gz_send, gz_recv, gz_sem, 0, 0, partner)
    arrive(gz_recv, gz_sem, 0)
    sums = sums + gz_recv[...].astype(F32)
    gate, up = sums[0:SLOTS], sums[SLOTS : 2 * SLOTS]
    act[me_q] = (gate / (1.0 + jnp.exp(-gate)) * up).astype(BF16)
    def add(total, q):
        rows_q = pl.ds(pl.multiple_of(q * LANES, LANES), LANES)
        return total + dot(act[q], wd_t[rows_q, :], 1, 0)

    total = spread(act, act_sem, add, jnp.zeros((SLOTS, COLS), F32))
    down[:, 0:COLS] = total

    result = jnp.concatenate([down[:, q * LANES : (q + 1) * LANES] for q in range(QS)], axis=0)
    packed = dot(perm_t[...], result.astype(BF16), 1, 0).astype(BF16)
    ret[...] = packed.reshape(NCTX, QS * CAP, LANES)
    to_all(ret, ret_recv, r_sem)
    from_all(ret_recv, r_sem)
    returned = ret_recv[...].reshape(PAD, LANES)
    high, low = split(pick_weight)
    final = (hidden + dot(high, returned, 1, 0) + dot(low, returned, 1, 0)).astype(BF16)
    for q in range(QS):
        width = min(LANES, COLS - q * LANES)
        out[:, q * LANES : q * LANES + width] = final[q * ROW_DEV : (q + 1) * ROW_DEV, 0:width]

    for src, sems, n in sent:
        pltpu.make_async_remote_copy(
            src_ref=src, dst_ref=src, send_sem=sems.at[0, n], recv_sem=sems.at[1, n],
            device_id=partner, device_id_type=MESH,
        ).wait_send()


def per_device(
    q_nope, q_rope, w_uk, w_uv, prompt, w_out, residual, routes, route_scores,
    expert_gate, expert_up, expert_down,
):
    vmem, hbm = pl.BlockSpec(memory_space=pltpu.VMEM), pl.BlockSpec(memory_space=pl.ANY)
    dma = pltpu.SemaphoreType.DMA
    near = 2 * NX
    half = VDIM // 2
    scratch = [
        ((ROW_DEV, COLS), BF16),
        ((ROW_DEV, TOPK), jnp.int32),
        ((ROW_DEV, TOPK), F32),
        ((ROWS * HEADS, NOPE), BF16),
        ((ROWS * HEADS, NOPE), F32),
        ((HEADS, ROPE, ROWS), BF16),
        ((HEADS, NOPE, LAT), BF16),
        ((HEADS, LAT, VDIM), BF16),
        ((LAT + ROPE, KEYS), BF16),
        ((KEYS, LAT + ROPE), BF16),
        ((COLS, HEADS * VDIM), BF16),
        ((HEADS * VDIM, COLS), BF16),
        ((PAD, 2 * FF), BF16),
        ((COLS, FF), BF16),
        ((FF, COLS), BF16),
        ((PAD, PAD), BF16),
        ((PAD, PAD), BF16),
        ((HEADS, 2, half, ROWS), BF16),
        ((HEADS, 8, LANES), F32),
        ((near, half, ROWS), BF16),
        ((near, 8, LANES), F32),
        ((half, ROWS), BF16),
        ((half, ROWS), BF16),
        ((8, LANES), F32),
        ((8, LANES), F32),
        ((near, half, ROWS), BF16),
        ((ROWS, PAD), F32),
        ((NY, 2, ROWS // 2, LANES), BF16),
        ((NY, 2, ROWS // 2, LANES), BF16),
        ((2, HALF_Z, QS * ROW_DEV, LANES), BF16),
        ((NZ, QS * ROW_DEV, LANES), BF16),
        ((ROW_DEV, PAD), F32),
        ((NCTX, QS * CAP, LANES), BF16),
        ((NCTX, QS * CAP, LANES), BF16),
        ((NX, 2 * SLOTS, LANES), F32),
        ((NX, 2 * SLOTS, LANES), BF16),
        ((NX, 2 * SLOTS, LANES), BF16),
        ((NX, 2 * SLOTS, LANES), BF16),
        ((NX, 2 * SLOTS, LANES), BF16),
        ((2 * SLOTS, LANES), BF16),
        ((2 * SLOTS, LANES), BF16),
        ((near, SLOTS, LANES), BF16),
        ((SLOTS, PAD), F32),
        ((NCTX, QS * CAP, LANES), BF16),
        ((NCTX, QS * CAP, LANES), BF16),
    ]
    sems = [(12,)] + [(2, n) for n in (near, near, 2, near, 2 * NY, NZ, NCTX, NX, NX, 1, near, NCTX)]
    return pl.pallas_call(
        kernel,
        out_shape=pltpu.VMEM((ROW_DEV, COLS), BF16),
        in_specs=[hbm] * 12,
        out_specs=vmem,
        scratch_shapes=[pltpu.VMEM(*s) for s in scratch] + [dma(s) for s in sems],
        compiler_params=pltpu.CompilerParams(
            collective_id=0, has_side_effects=True, vmem_limit_bytes=60 * 2**20
        ),
        name="layer",
    )(
        residual, routes, route_scores,
        q_nope.reshape(ROWS * HEADS, NOPE), jnp.transpose(q_rope, (1, 2, 0)), w_uk, w_uv, prompt.T,
        w_out.T, expert_gate[0], expert_up[0], expert_down[0].T,
    )


def solution(mesh):
    in_specs = (
        P(None, "ctx", None),
        P(None, "ctx", None),
        P("ctx", None, None),
        P("ctx", None, None),
        P("grp", None),
        P("ctx", "grp"),
        P("ctx", "grp"),
        P("ctx", None),
        P("ctx", None),
        P("ctx", "grp", None),
        P("ctx", "grp", None),
        P("ctx", None, "grp"),
    )
    return jax.shard_map(
        per_device, mesh=mesh, in_specs=in_specs, out_specs=P("ctx", "grp"), check_vma=False
    )
```

```python
import jax
import jax.numpy as jnp
from jax import lax
from jax.experimental import pallas as pl
from jax.experimental.pallas import tpu as pltpu
from jax.sharding import PartitionSpec as P

NOPE = 128
ROPE = 64
LAT = 512
VDIM = 128
CAP = 4
TOPK = 8
FF = 1024
ROWS = 256
HEADS = 4
KEYS = 384
COLS = 448
LANES = 128
PAD = 512
QS = PAD // LANES
ROW_DEV = 8
HALF_Z = 4
NZ, NY, NX = 8, 4, 4
NCTX = NZ * NY
SLOTS = NCTX * CAP
ROUTE_FACTOR = 2.5
FAR_FIRST = (2, 1, 3, 0)
OFFSETS = [(dz, dy) for dz in (4, 3, 5, 2, 6, 1, 7, 0) for dy in FAR_FIRST][:-1]
F32 = jnp.float32
BF16 = jnp.bfloat16
MESH = pl.DeviceIdType.MESH


def dot(a, b, ca, cb):
    return lax.dot_general(a, b, (((ca,), (cb,)), ((), ())), preferred_element_type=F32)


def split(a):
    high = a.astype(BF16)
    return high, (a - high.astype(F32)).astype(BF16)


def kernel(
    residual_hbm, routes_hbm, scores_hbm,
    qn_hbm, qr_hbm, w_uk_hbm, w_uv_hbm, prompt_hbm, w_out_hbm, wg_hbm, wu_hbm, wd_hbm,
    out,
    residual, routes, scores,
    qn, q_wide, qr, w_uk, w_uv, prompt, keys,
    w_out, w_out_t, wgu, wd, wd_t, perm, perm_t,
    obuf, lse, o_recv, l_recv, zh_send, zh_recv, zl_send, zl_recv, att,
    proj, pbuf, p_recv, zbuf, z_recv, res_pad, disp, arrived,
    gu_own, gu_send, gu_recv, gx_send, gx_recv, gz_send, gz_recv, act, down, ret, ret_recv, parts_high, parts_low,
    load_sem, o_sem, l_sem, zh_sem, ag_sem, y_sem, z_sem, d_sem, gs_sem, g_sem, gz_sem, act_sem, r_sem,
):
    me_c = lax.axis_index("ctx")
    me_g = lax.axis_index("grp")
    z, y = me_c // NY, me_c % NY
    x, zh, core = me_g // 4, (me_g // 2) % 2, me_g % 2
    me_q = x * 2 + core
    partner = {"grp": x * 4 + (1 - zh) * 2 + core}

    def near(d, c):
        return {"grp": ((x + d) % NX) * 4 + zh * 2 + c}

    barrier = pltpu.get_barrier_semaphore()
    sibling = near(0, 1 - core)
    others = [((z + dz) % NZ) * NY + (y + dy) % NY for dz, dy in OFFSETS]
    sources = [((z + NZ - dz) % NZ) * NY + (y + NY - dy) % NY for dz, dy in OFFSETS]
    greeted = [partner] + [{"ctx": c} for c in others]
    greeted += [near(d, c) for d in FAR_FIRST[:3] for c in range(2)] + [sibling]
    for device in greeted:
        pl.semaphore_signal(barrier, inc=1, device_id=device, device_id_type=MESH)
    pairs = (
        (prompt_hbm, prompt),
        (qn_hbm, qn),
        (w_uk_hbm, w_uk),
        (qr_hbm, qr),
        (w_uv_hbm, w_uv),
        (w_out_hbm, w_out),
        (wg_hbm, wgu.at[pl.ds(0, COLS), pl.ds(0, FF)]),
        (wu_hbm, wgu.at[pl.ds(0, COLS), pl.ds(FF, FF)]),
        (wd_hbm, wd),
        (residual_hbm, residual),
        (routes_hbm, routes),
        (scores_hbm, scores),
    )
    loads = [pltpu.make_async_copy(a, b, load_sem.at[i]) for i, (a, b) in enumerate(pairs)]
    for load in loads[0:5]:
        load.start()
    sent = []

    def send(src, dst, sems, n, at, device):
        copy = pltpu.make_async_remote_copy(
            src_ref=src, dst_ref=dst, send_sem=sems.at[0, n], recv_sem=sems.at[1, at],
            device_id=device, device_id_type=MESH,
        )
        copy.start()
        sent.append((src, sems, n))

    def arrive(dst, sems, at):
        pltpu.make_async_remote_copy(
            src_ref=dst, dst_ref=dst, send_sem=sems.at[0, at], recv_sem=sems.at[1, at],
            device_id=partner, device_id_type=MESH,
        ).wait_recv()

    def spread(buf, sems, use=lambda total, q: total, total=0):
        for d in (2, 1, 3):
            send(buf.at[me_q], buf.at[me_q], sems, d, d, near(d, core))
        send(buf.at[me_q], buf.at[me_q], sems, NX, NX, sibling)
        for d in (1, 3, 2):
            got = ((x + NX - d) % NX) * 2 + core
            arrive(buf.at[got], sems, d)
            send(buf.at[got], buf.at[got], sems, NX + d, NX + d, sibling)
        for d in (0, 1, 3, 2):
            total = use(total, ((x + NX - d) % NX) * 2 + core)
        for d in (0, 1, 3, 2):
            got = ((x + NX - d) % NX) * 2 + 1 - core
            arrive(buf.at[got], sems, NX + d)
            total = use(total, got)
        return total

    def fold(v):
        return jnp.concatenate([v[:, 0:LANES], v[:, LANES:ROWS]] * 4, axis=0)

    def unfold(v):
        return jnp.concatenate([v[0:1], v[1:2]], axis=1)

    scale = (NOPE + ROPE) ** -0.5
    loads[0].wait()
    keys[...] = prompt[...].T
    loads[1].wait()
    q_wide[...] = qn[...].astype(F32)
    for load in loads[2:5]:
        load.wait()
    for load in loads[5:12]:
        load.start()
    for h in range(HEADS):
        q = q_wide[pl.ds(h, ROWS, stride=HEADS), :].astype(BF16)
        queries = jnp.concatenate([dot(w_uk[h], q, 0, 1).astype(BF16), qr[h]], axis=0)
        s = dot(keys[...], queries, 1, 0) * scale
        top = jnp.max(s, axis=0, keepdims=True)
        raised = jnp.exp(s - top)
        total = jnp.sum(raised, axis=0, keepdims=True)
        weighted = dot(prompt[0:LAT, :], raised.astype(BF16), 1, 0)
        high, low = split(weighted)
        values = dot(w_uv[h], high, 0, 0) + dot(w_uv[h], low, 0, 0)
        o = (values / total).astype(BF16)
        obuf[h] = o.reshape(2, VDIM // 2, ROWS)
        lse[h] = fold(top + jnp.log(total))
    pl.semaphore_wait(barrier, len(greeted))
    for d in FAR_FIRST:
        h = (x + d) % NX
        for c in range(2) if d else (1 - core,):
            send(obuf.at[h, c], o_recv.at[d * 2 + core], o_sem, d * 2 + c, d * 2 + core, near(d, c))
            send(lse.at[h], l_recv.at[d * 2 + core], l_sem, d * 2 + c, d * 2 + core, near(d, c))
    o_recv[core] = obuf[x, core]
    l_recv[core] = lse[x]

    wgu[COLS:PAD, :] = jnp.zeros((PAD - COLS, 2 * FF), BF16)
    slot = lax.broadcasted_iota(jnp.int32, (PAD, PAD), 0)
    place = lax.broadcasted_iota(jnp.int32, (PAD, PAD), 1)

    def place_of(k):
        k2 = k % SLOTS
        return (k2 // CAP) * (QS * CAP) + (k // SLOTS) * CAP + k2 % CAP

    perm[...] = jnp.where(place_of(slot) == place, 1.0, 0.0).astype(BF16)
    perm_t[...] = jnp.where(place_of(place) == slot, 1.0, 0.0).astype(BF16)
    for load in loads[9:12]:
        load.wait()
    res_pad[...] = jnp.zeros((ROW_DEV, PAD), F32)
    res_pad[:, 0:COLS] = residual[...].astype(F32)
    proj[:, PAD - LANES : PAD] = jnp.zeros((ROWS, LANES), F32)
    down[:, PAD - LANES : PAD] = jnp.zeros((SLOTS, LANES), F32)

    lane = lax.broadcasted_iota(jnp.int32, (ROW_DEV, PAD), 1)
    expert_of = lane // (QS * CAP)
    scored = scores[...]
    gate_weights = ROUTE_FACTOR * scored / jnp.sum(scored, axis=1, keepdims=True)
    chosen = jnp.zeros((ROW_DEV, PAD), F32)
    weight = jnp.zeros((ROW_DEV, PAD), F32)
    for k in range(TOPK):
        hit = routes[:, k : k + 1] == expert_of
        chosen = chosen + jnp.where(hit, 1.0, 0.0)
        weight = weight + jnp.where(hit, gate_weights[:, k : k + 1], 0.0)
    row = lax.broadcasted_iota(jnp.int32, (ROW_DEV, PAD), 0)
    before = jnp.zeros((ROW_DEV, PAD), F32)
    for r in range(ROW_DEV - 1):
        before = before + jnp.where(row > r, chosen[r : r + 1, :], 0.0)
    picked = jnp.where(before == (lane % CAP).astype(F32), chosen, 0.0)
    block_of = (lane // CAP) % QS
    pick = jnp.concatenate([jnp.where(block_of == q, picked, 0.0) for q in range(QS)], axis=0)
    pick_weight = jnp.concatenate(
        [jnp.where(block_of == q, picked * weight, 0.0) for q in range(QS)], axis=0
    )

    for zz in range(NZ):
        some = pick_weight[:, zz * NY * QS * CAP : (zz + 1) * NY * QS * CAP]
        parts_high[zz], parts_low[zz] = split(some)
    loads[5].wait()
    w_out_t[...] = w_out[...].T

    for d in FAR_FIRST:
        for c in range(2) if d else (1 - core,):
            arrive(o_recv.at[d * 2 + c], o_sem, d * 2 + c)
            arrive(l_recv.at[d * 2 + c], l_sem, d * 2 + c)

    def merge(outs, sums):
        top = sums[0]
        for v in sums[1:]:
            top = jnp.maximum(top, v)
        scaled = [jnp.exp(v - top) for v in sums]
        total = scaled[0]
        for v in scaled[1:]:
            total = total + v
        o = jnp.zeros(outs[0].shape, F32)
        for v, s in zip(outs, scaled):
            o = o + v.astype(F32) * s
        return o / total, top + jnp.log(total)

    o, l = merge([o_recv[i] for i in range(2 * NX)], [unfold(l_recv[i]) for i in range(2 * NX)])
    zh_send[...] = o.astype(BF16)
    zl_send[...] = fold(l)
    send(zh_send, zh_recv, zh_sem, 0, 0, partner)
    send(zl_send, zl_recv, zh_sem, 1, 1, partner)
    loads[8].wait()
    wd_t[...] = wd[...].T
    arrive(zh_recv, zh_sem, 0)
    arrive(zl_recv, zh_sem, 1)
    o, _ = merge([zh_send[...], zh_recv[...]], [l, unfold(zl_recv[...])])
    att[me_q] = o.astype(BF16)
    spread(att, ag_sem)

    proj[:, 0:COLS] = dot(att[...].reshape(HEADS * VDIM, ROWS), w_out_t[...], 0, 0)
    for to in range(NY):
        parts = []
        for q in range(QS):
            part = proj[:, q * LANES : (q + 1) * LANES].reshape(NZ, NY, ROW_DEV, LANES)
            parts.append(part[:, to])
        block = jnp.stack(parts, axis=1).reshape(2, HALF_Z * QS * ROW_DEV, LANES)
        pbuf[to] = block.astype(BF16)
    halves = (1 - z // HALF_Z, z // HALF_Z)
    for k, half in enumerate(halves):
        for d in (2, 1, 3):
            to = (y + d) % NY
            device = {"ctx": z * NY + to}
            send(pbuf.at[to, half], p_recv.at[d, k], y_sem, d * 2 + k, d * 2 + k, device)
    for k, half in enumerate(halves):
        total = pbuf[y, half].astype(F32)
        for d in (1, 3, 2):
            arrive(p_recv.at[d, k], y_sem, d * 2 + k)
            total = total + p_recv[d, k].astype(F32)
        zbuf[half] = total.reshape(HALF_Z, QS * ROW_DEV, LANES).astype(BF16)
        for j in range(HALF_Z)[k:]:
            at = (z + j) % HALF_Z
            device = {"ctx": (half * HALF_Z + at) * NY + y}
            n = j + HALF_Z * (1 - k)
            send(zbuf.at[half, at], z_recv.at[n], z_sem, n, n, device)
    hidden = jnp.concatenate([res_pad[:, q * LANES : (q + 1) * LANES] for q in range(QS)], axis=0)
    hidden = hidden + zbuf[halves[1], z % HALF_Z].astype(F32)
    for d in range(1, NZ):
        arrive(z_recv.at[d], z_sem, d)
        hidden = hidden + z_recv[d].astype(F32)

    outgoing = dot(pick.astype(BF16), hidden.astype(BF16), 0, 0).astype(BF16)
    disp[...] = outgoing.reshape(NCTX, QS * CAP, LANES)
    def to_all(src, dst, sems):
        dst[me_c] = src[me_c]
        for n, to in enumerate(others):
            send(src.at[to], dst.at[me_c], sems, n, n, {"ctx": to})

    def from_all(dst, sems):
        for n, source in enumerate(sources):
            arrive(dst.at[source], sems, n)

    to_all(disp, arrived, d_sem)
    loads[6].wait()
    loads[7].wait()
    from_all(arrived, d_sem)
    rows = dot(perm[...], arrived[...].reshape(PAD, LANES), 1, 0).astype(BF16)
    rows = jnp.concatenate([rows[q * SLOTS : (q + 1) * SLOTS] for q in range(QS)], axis=1)

    wide = 2 * LANES
    for d in FAR_FIRST:
        first = pl.multiple_of(((x + d) % NX) * wide, wide)
        gate = dot(rows, wgu[:, pl.ds(first, wide)], 1, 0)
        up = dot(rows, wgu[:, pl.ds(FF + first, wide)], 1, 0)
        even = jnp.concatenate([gate[:, 0:LANES], up[:, 0:LANES]], axis=0)
        odd = jnp.concatenate([gate[:, LANES:wide], up[:, LANES:wide]], axis=0)
        gu_own[d] = jnp.where(core == 0, even, odd)
        gu_send[d] = jnp.where(core == 0, odd, even).astype(BF16)
        send(gu_send.at[d], gu_recv.at[d], gs_sem, d, d, sibling)
    for d in (2, 1, 3):
        arrive(gu_recv.at[d], gs_sem, d)
        gx_send[d] = (gu_own[d] + gu_recv[d].astype(F32)).astype(BF16)
        send(gx_send.at[d], gx_recv.at[d], g_sem, d, d, near(d, core))
    arrive(gu_recv.at[0], gs_sem, 0)
    sums = gu_own[0] + gu_recv[0].astype(F32)
    for d in (1, 3, 2):
        arrive(gx_recv.at[d], g_sem, d)
        sums = sums + gx_recv[d].astype(F32)
    gz_send[...] = sums.astype(BF16)
    send(gz_send, gz_recv, gz_sem, 0, 0, partner)
    arrive(gz_recv, gz_sem, 0)
    sums = sums + gz_recv[...].astype(F32)
    gate, up = sums[0:SLOTS], sums[SLOTS : 2 * SLOTS]
    act[me_q] = (gate / (1.0 + jnp.exp(-gate)) * up).astype(BF16)
    def add(total, q):
        rows_q = pl.ds(pl.multiple_of(q * LANES, LANES), LANES)
        return total + dot(act[q], wd_t[rows_q, :], 1, 0)

    total = spread(act, act_sem, add, jnp.zeros((SLOTS, COLS), F32))
    down[:, 0:COLS] = total

    result = jnp.concatenate([down[:, q * LANES : (q + 1) * LANES] for q in range(QS)], axis=0)
    packed = dot(perm_t[...], result.astype(BF16), 1, 0).astype(BF16)
    ret[...] = packed.reshape(NCTX, QS * CAP, LANES)
    to_all(ret, ret_recv, r_sem)
    for g in range(NZ):
        for n in range(g * NY, min(g * NY + NY, len(sources))):
            arrive(ret_recv.at[sources[n]], r_sem, n)
        at = (z + NZ - OFFSETS[g * NY][0]) % NZ
        group = ret_recv[pl.ds(at * NY, NY)].reshape(NY * QS * CAP, LANES)
        hidden = hidden + dot(parts_high[at], group, 1, 0) + dot(parts_low[at], group, 1, 0)
    final = hidden.astype(BF16)
    for q in range(QS):
        width = min(LANES, COLS - q * LANES)
        out[:, q * LANES : q * LANES + width] = final[q * ROW_DEV : (q + 1) * ROW_DEV, 0:width]

    for src, sems, n in sent:
        pltpu.make_async_remote_copy(
            src_ref=src, dst_ref=src, send_sem=sems.at[0, n], recv_sem=sems.at[1, n],
            device_id=partner, device_id_type=MESH,
        ).wait_send()


def per_device(
    q_nope, q_rope, w_uk, w_uv, prompt, w_out, residual, routes, route_scores,
    expert_gate, expert_up, expert_down,
):
    vmem, hbm = pl.BlockSpec(memory_space=pltpu.VMEM), pl.BlockSpec(memory_space=pl.ANY)
    dma = pltpu.SemaphoreType.DMA
    near = 2 * NX
    half = VDIM // 2
    scratch = [
        ((ROW_DEV, COLS), BF16),
        ((ROW_DEV, TOPK), jnp.int32),
        ((ROW_DEV, TOPK), F32),
        ((ROWS * HEADS, NOPE), BF16),
        ((ROWS * HEADS, NOPE), F32),
        ((HEADS, ROPE, ROWS), BF16),
        ((HEADS, NOPE, LAT), BF16),
        ((HEADS, LAT, VDIM), BF16),
        ((LAT + ROPE, KEYS), BF16),
        ((KEYS, LAT + ROPE), BF16),
        ((COLS, HEADS * VDIM), BF16),
        ((HEADS * VDIM, COLS), BF16),
        ((PAD, 2 * FF), BF16),
        ((COLS, FF), BF16),
        ((FF, COLS), BF16),
        ((PAD, PAD), BF16),
        ((PAD, PAD), BF16),
        ((HEADS, 2, half, ROWS), BF16),
        ((HEADS, 8, LANES), F32),
        ((near, half, ROWS), BF16),
        ((near, 8, LANES), F32),
        ((half, ROWS), BF16),
        ((half, ROWS), BF16),
        ((8, LANES), F32),
        ((8, LANES), F32),
        ((near, half, ROWS), BF16),
        ((ROWS, PAD), F32),
        ((NY, 2, ROWS // 2, LANES), BF16),
        ((NY, 2, ROWS // 2, LANES), BF16),
        ((2, HALF_Z, QS * ROW_DEV, LANES), BF16),
        ((NZ, QS * ROW_DEV, LANES), BF16),
        ((ROW_DEV, PAD), F32),
        ((NCTX, QS * CAP, LANES), BF16),
        ((NCTX, QS * CAP, LANES), BF16),
        ((NX, 2 * SLOTS, LANES), F32),
        ((NX, 2 * SLOTS, LANES), BF16),
        ((NX, 2 * SLOTS, LANES), BF16),
        ((NX, 2 * SLOTS, LANES), BF16),
        ((NX, 2 * SLOTS, LANES), BF16),
        ((2 * SLOTS, LANES), BF16),
        ((2 * SLOTS, LANES), BF16),
        ((near, SLOTS, LANES), BF16),
        ((SLOTS, PAD), F32),
        ((NCTX, QS * CAP, LANES), BF16),
        ((NCTX, QS * CAP, LANES), BF16),
        ((NZ, QS * ROW_DEV, NY * QS * CAP), BF16),
        ((NZ, QS * ROW_DEV, NY * QS * CAP), BF16),
    ]
    sems = [(12,)] + [(2, n) for n in (near, near, 2, near, 2 * NY, NZ, NCTX, NX, NX, 1, near, NCTX)]
    return pl.pallas_call(
        kernel,
        out_shape=pltpu.VMEM((ROW_DEV, COLS), BF16),
        in_specs=[hbm] * 12,
        out_specs=vmem,
        scratch_shapes=[pltpu.VMEM(*s) for s in scratch] + [dma(s) for s in sems],
        compiler_params=pltpu.CompilerParams(
            collective_id=0, has_side_effects=True, vmem_limit_bytes=60 * 2**20
        ),
        name="layer",
    )(
        residual, routes, route_scores,
        q_nope.reshape(ROWS * HEADS, NOPE), jnp.transpose(q_rope, (1, 2, 0)), w_uk, w_uv, prompt.T,
        w_out.T, expert_gate[0], expert_up[0], expert_down[0].T,
    )


def solution(mesh):
    in_specs = (
        P(None, "ctx", None),
        P(None, "ctx", None),
        P("ctx", None, None),
        P("ctx", None, None),
        P("grp", None),
        P("ctx", "grp"),
        P("ctx", "grp"),
        P("ctx", None),
        P("ctx", None),
        P("ctx", "grp", None),
        P("ctx", "grp", None),
        P("ctx", None, "grp"),
    )
    return jax.shard_map(
        per_device, mesh=mesh, in_specs=in_specs, out_specs=P("ctx", "grp"), check_vma=False
    )
```
